32 devices in a mesh: seq: 8 (over z, x), rep: 4 (over y, core).
Axes of the slice: x: 2, y: 2, z: 4, core: 2. Of those that a mesh axis runs over, the one named last changes fastest.
Arguments:
- tokens: bfloat16 [4096, 2304], P(('rep', 'seq')), parts along dimension 0, may hold values from -6 to 6
- qkv_weight: bfloat16 [2304, 6144], P(None, 'seq'), may hold values from -0.125 to 0.125
- conv_weight: float32 [4, 6144], replicated, may hold values from -3 to 3
- decay_down: bfloat16 [2304, 128], replicated, may hold values from -0.125 to 0.125
- decay_up: bfloat16 [128, 2048], replicated, may hold values from -0.5 to 0.5
- decay_rate: float32 [2048], replicated, may hold values from 0.0009765625 to 0.1
- beta_weight: bfloat16 [2304, 16], replicated, may hold values from -0.125 to 0.125
- beta_scale: float32 [16], replicated, may hold values from 0.125 to 1
- gate_down: bfloat16 [2304, 128], replicated, may hold values from -0.125 to 0.125
- gate_up: bfloat16 [128, 2048], replicated, may hold values from -0.5 to 0.5
- norm_gain: float32 [128], replicated, may hold values from 0.1 to 1.9
Outputs:
- attended: bfloat16 [4096, 2048], P(('rep', 'seq')), parts along dimension 0
The draws below stay inside these ranges and needn't reach their ends.
There are 4 independent parts, one for each index of `rep`. The reference program is written for one: setup_inputs(seed, part) draws one part's arguments, and reference() takes and returns one part's arrays. A program takes and returns all parts, laid end to end along the dimension named above; an argument that names none is the same for every part. Nothing has to cross between parts.
All inputs are finite; a program needn't handle non-finite values.
Results may differ from the reference program's by a relative error of at most 0.0054.
Values may be sent and summed in bfloat16 or wider, within the bound.
A program may use at most 192 MiB of HBM per device.

```python
import math
import jax
import jax.numpy as jnp
from jax import lax

D = 2304
H = 16
DK = 128
RANK = 128
CONV = 4
BLOCK = 64
TOKENS = 1024
HV = 2048


def draw_beta_scale(key, part):
    picker = jax.random.fold_in(key, 11)
    spread_key = jax.random.fold_in(key, 12)
    upper_key = jax.random.fold_in(key, 13)
    order = jax.random.permutation(picker, H)
    lasting = order >= H // 2
    level = jnp.exp(jax.random.uniform(spread_key, (H,), jnp.float32, 0.0, math.log(4.0)))
    quick = jax.random.uniform(upper_key, (H,), jnp.float32, 0.5, 1.0)
    return jnp.where(lasting, level * (DK / TOKENS), quick).astype(jnp.float32)


def block_levels(key, shape, split, smallest, high):
    gain = 1.0
    for position, parts in split:
        draws = jax.random.uniform(jax.random.fold_in(jax.random.fold_in(key, 6), position), (parts,), jnp.float32, smallest / len(split), high / len(split))
        gain = gain * jnp.repeat(jnp.exp(draws), shape[position] // parts).reshape((-1,) + (1,) * (len(shape) - 1 - position))
    return gain


def scatter_about(own_key, dims, deviation, most, split=(), kind=jnp.bfloat16):
    drawn = deviation * jax.random.normal(own_key, dims, jnp.float32)
    if split:
        drawn = drawn * block_levels(own_key, dims, split, -0.22, 0.18)
    return jnp.clip(drawn, -most, most).astype(kind)


def setup_inputs(seed: int = 0, part: int = 0) -> dict:
    streams_of = jax.random.split(jax.random.key(seed), 12)
    part_keys = jax.random.split(jax.random.fold_in(streams_of[11], part), 12)
    tokens = scatter_about(part_keys[0], (TOKENS, D), 1.0, 6.0, ((0, 8),))
    qkv_weight = scatter_about(streams_of[1], (D, 3 * HV), D ** -0.5, 0.125, ((1, 8),))
    conv_weight = scatter_about(streams_of[2], (CONV, 3 * HV), 0.5, 3.0, (), jnp.float32)
    decay_down = scatter_about(streams_of[3], (D, RANK), D ** -0.5, 0.125)
    decay_up = scatter_about(streams_of[4], (RANK, HV), RANK ** -0.5, 0.5)
    decay_rate = jnp.clip(jnp.exp(jax.random.uniform(streams_of[5], (HV,), jnp.float32, math.log(0.0009765625), math.log(0.1))), 0.0009765625, 0.1)
    beta_weight = scatter_about(streams_of[6], (D, H), D ** -0.5, 0.125)
    beta_scale = draw_beta_scale(jax.random.fold_in(streams_of[11], 71), part)
    gate_down = scatter_about(streams_of[8], (D, RANK), D ** -0.5, 0.125)
    gate_up = scatter_about(streams_of[9], (RANK, HV), RANK ** -0.5, 0.5)
    norm_gain = jnp.clip(1.0 + 0.18 * jax.random.normal(streams_of[10], (DK,), jnp.float32), 0.1, 1.9)
    return {"tokens": tokens, "qkv_weight": qkv_weight, "conv_weight": conv_weight, "decay_down": decay_down, "decay_up": decay_up, "decay_rate": decay_rate, "beta_weight": beta_weight, "beta_scale": beta_scale, "gate_down": gate_down, "gate_up": gate_up, "norm_gain": norm_gain}


precise = lax.Precision.HIGHEST

def unit_rows(vector):
    return vector * lax.rsqrt(lax.optimization_barrier(jnp.sum(vector * vector, axis=-1, keepdims=True)) + 1e-06)

def features(padded, count, conv_weight):
    combined = conv_weight[0] * padded[0:count].astype(jnp.float32)
    for offset in range(1, CONV):
        combined = combined + conv_weight[offset] * padded[offset:offset + count].astype(jnp.float32)
    active = jax.nn.silu(combined).reshape(count, 3, H, DK)
    query = unit_rows(active[:, 0]) * DK ** (-0.5)
    keys = unit_rows(active[:, 1])
    values = active[:, 2]
    return (query, keys, values)

def gates(tokens, decay_down, decay_up, decay_rate, beta_weight, beta_scale, gate_down, gate_up):
    beta = beta_scale * jax.nn.sigmoid(jnp.dot(tokens.astype(jnp.float32), beta_weight.astype(jnp.float32), preferred_element_type=jnp.float32))
    decay_low = jnp.dot(tokens.astype(jnp.float32), decay_down.astype(jnp.float32), preferred_element_type=jnp.float32).astype(jnp.bfloat16)
    logdec = -decay_rate * jax.nn.sigmoid(jnp.dot(decay_low.astype(jnp.float32), decay_up.astype(jnp.float32), preferred_element_type=jnp.float32))
    gate_low = jnp.dot(tokens.astype(jnp.float32), gate_down.astype(jnp.float32), preferred_element_type=jnp.float32).astype(jnp.bfloat16)
    gate_value = jax.nn.sigmoid(jnp.dot(gate_low.astype(jnp.float32), gate_up.astype(jnp.float32), preferred_element_type=jnp.float32))
    return (beta, logdec, gate_value)

def to_blocks(array, count):
    return array.reshape(count // BLOCK, BLOCK, H, array.shape[-1]).transpose(0, 2, 1, 3)

def block_terms(query, keys, values, beta, logdec):
    log_sum = jnp.cumsum(logdec, axis=2)
    grow = jnp.exp(log_sum)
    keys_up = keys * grow
    keys_down = keys * jnp.exp(-log_sum)
    query_up = query * grow
    keys_end = keys * jnp.exp(log_sum[:, :, -1:, :] - log_sum)
    length = query.shape[2]
    rows = lax.broadcasted_iota(jnp.int32, (length, length), 0)
    columns = lax.broadcasted_iota(jnp.int32, (length, length), 1)
    scores = jnp.einsum('nhic,nhjc->nhij', keys_up, keys_down, precision=precise) * beta[..., None]
    system = jnp.where(rows > columns, scores, 0.0) + jnp.eye(length, dtype=jnp.float32)
    right_side = jnp.concatenate([values, keys_up], axis=-1) * beta[..., None]
    solved = jax.scipy.linalg.solve_triangular(system, right_side, lower=True, unit_diagonal=True)
    values_w = solved[..., :DK]
    keys_w = solved[..., DK:]
    attend = jnp.where(rows >= columns, jnp.einsum('nhic,nhjc->nhij', query_up, keys_down, precision=precise), 0.0)
    decay_end = jnp.exp(log_sum[:, :, -1, :])
    return (query_up, keys_end, values_w, keys_w, attend, decay_end)

def advance(state, inputs):
    query_up, keys_end, values_w, keys_w, attend, decay_end = inputs
    update = values_w - jnp.einsum('hcd,hde->hce', keys_w, state, precision=precise)
    output = jnp.einsum('hcd,hde->hce', query_up, state, precision=precise)
    output = output + jnp.einsum('hij,hje->hie', attend, update, precision=precise)
    state = decay_end[..., None] * state + jnp.einsum('hcd,hce->hde', keys_end, update, precision=precise)
    return (state, output)

def finish(core, gate_value, norm_gain, count):
    scaled = core * lax.rsqrt(lax.optimization_barrier(jnp.mean(core * core, axis=-1, keepdims=True)) + 1e-06) * norm_gain
    return (scaled.reshape(count, H * DK) * gate_value).astype(jnp.bfloat16)

def reference(tokens, qkv_weight, conv_weight, decay_down, decay_up, decay_rate, beta_weight, beta_scale, gate_down, gate_up, norm_gain):
    count = tokens.shape[0]
    mixed = jnp.dot(tokens.astype(jnp.float32), qkv_weight.astype(jnp.float32), preferred_element_type=jnp.float32).astype(jnp.bfloat16)
    padded = jnp.concatenate([jnp.zeros((CONV - 1, mixed.shape[1]), jnp.bfloat16), mixed], axis=0)
    query, keys, values = features(padded, count, conv_weight)
    beta, logdec, gate_value = gates(tokens, decay_down, decay_up, decay_rate, beta_weight, beta_scale, gate_down, gate_up)
    beta_blocks = beta.reshape(count // BLOCK, BLOCK, H).transpose(0, 2, 1)
    terms = block_terms(to_blocks(query, count), to_blocks(keys, count), to_blocks(values, count), beta_blocks, to_blocks(logdec.reshape(count, H, DK), count))
    initial = jnp.zeros((H, DK, DK), jnp.float32)
    final_state, outputs = lax.scan(advance, initial, terms)
    core = outputs.transpose(0, 2, 1, 3).reshape(count, H, DK)
    return finish(core, gate_value, norm_gain, count)
```

```python
import functools
import jax
import jax.numpy as jnp
from jax import lax
from jax.experimental import pallas as pl
from jax.experimental.pallas import tpu as pltpu
from jax.sharding import PartitionSpec as P

H = 16
DK = 128
CONV = 4
BLOCK = 64


precise = lax.Precision.HIGHEST


def from_behind(block, axis, distance):
    devices = range(lax.axis_size(axis))
    route = [(i - distance, i) for i in devices if i - distance in devices]
    return lax.ppermute(block, axis, route)


def carried_in(x, axis, combine, identity):
    devices, mine = (lax.axis_size(axis), lax.axis_index(axis))
    everything = jax.tree.map(lambda part: lax.all_gather(part, axis), x)
    start = jax.tree.map(
        lambda part, zero: jnp.broadcast_to(jnp.asarray(zero, part.dtype), part.shape), x, identity
    )

    def lap(k, before):
        reached = k < mine
        new = combine(before, jax.tree.map(lambda part: part[k], everything))
        return jax.tree.map(lambda a, b: jnp.where(reached, a, b), new, before)

    return lax.fori_loop(0, devices, lap, start)


def unit_rows(vector):
    return vector * lax.rsqrt(jnp.sum(vector * vector, axis=-1, keepdims=True) + 1e-06)


def features(padded, count, conv_weight):
    combined = conv_weight[0] * padded[0:count].astype(jnp.float32)
    for offset in range(1, CONV):
        combined = combined + conv_weight[offset] * padded[offset : offset + count].astype(
            jnp.float32
        )
    active = jax.nn.silu(combined).reshape(count, 3, H, DK)
    query = unit_rows(active[:, 0]) * DK ** (-0.5)
    keys = unit_rows(active[:, 1])
    values = active[:, 2]
    return (query, keys, values)


def gates(tokens, decay_down, decay_up, decay_rate, beta_weight, beta_scale, gate_down, gate_up):
    beta = beta_scale * jax.nn.sigmoid(
        jnp.dot(tokens, beta_weight, preferred_element_type=jnp.float32)
    )
    decay_low = jnp.dot(tokens, decay_down, preferred_element_type=jnp.float32).astype(jnp.bfloat16)
    logdec = -decay_rate * jax.nn.sigmoid(
        jnp.dot(decay_low, decay_up, preferred_element_type=jnp.float32)
    )
    gate_low = jnp.dot(tokens, gate_down, preferred_element_type=jnp.float32).astype(jnp.bfloat16)
    gate_value = jax.nn.sigmoid(jnp.dot(gate_low, gate_up, preferred_element_type=jnp.float32))
    return (beta, logdec, gate_value)


def to_blocks(array, count):
    return array.reshape(count // BLOCK, BLOCK, H, array.shape[-1]).transpose(0, 2, 1, 3)


def block_terms(query, keys, values, beta, logdec):
    log_sum = jnp.cumsum(logdec, axis=2)
    grow = jnp.exp(log_sum)
    keys_up = keys * grow
    keys_down = keys * jnp.exp(-log_sum)
    query_up = query * grow
    keys_end = keys * jnp.exp(log_sum[:, :, -1:, :] - log_sum)
    length = query.shape[2]
    rows = lax.broadcasted_iota(jnp.int32, (length, length), 0)
    columns = lax.broadcasted_iota(jnp.int32, (length, length), 1)
    scores = jnp.einsum("nhic,nhjc->nhij", keys_up, keys_down, precision=precise) * beta[..., None]
    system = jnp.where(rows > columns, scores, 0.0) + jnp.eye(length, dtype=jnp.float32)
    right_side = jnp.concatenate([values, keys_up], axis=-1) * beta[..., None]
    solved = jax.scipy.linalg.solve_triangular(system, right_side, lower=True, unit_diagonal=True)
    values_w = solved[..., :DK]
    keys_w = solved[..., DK:]
    attend = jnp.where(
        rows >= columns, jnp.einsum("nhic,nhjc->nhij", query_up, keys_down, precision=precise), 0.0
    )
    decay_end = jnp.exp(log_sum[:, :, -1, :])
    return (query_up, keys_end, values_w, keys_w, attend, decay_end)


def advance(state, inputs):
    query_up, keys_end, values_w, keys_w, attend, decay_end = inputs
    update = values_w - jnp.einsum("hcd,hde->hce", keys_w, state, precision=precise)
    output = jnp.einsum("hcd,hde->hce", query_up, state, precision=precise)
    output = output + jnp.einsum("hij,hje->hie", attend, update, precision=precise)
    state = decay_end[..., None] * state + jnp.einsum(
        "hcd,hce->hde", keys_end, update, precision=precise
    )
    return (state, output)


def matmul(left, right):
    return jnp.einsum("...de,...ef->...df", left, right, precision=precise)


def fold_block(carry, inputs):
    matrix, offset = carry
    keys_end, keys_w, values_w, decay_end = inputs
    eye_block = jnp.eye(DK, dtype=jnp.float32)
    block_matrix = decay_end[..., None] * eye_block - jnp.einsum(
        "hcd,hce->hde", keys_end, keys_w, precision=precise
    )
    block_offset = jnp.einsum("hcd,hce->hde", keys_end, values_w, precision=precise)
    return ((matmul(block_matrix, matrix), matmul(block_matrix, offset) + block_offset), None)


def join_pairs(first, second):
    return (matmul(second[0], first[0]), matmul(second[0], first[1]) + second[1])


def finish(core, gate_value, norm_gain, count):
    scaled = core * lax.rsqrt(jnp.mean(core * core, axis=-1, keepdims=True) + 1e-06) * norm_gain
    return (scaled.reshape(count, H * DK) * gate_value).astype(jnp.bfloat16)


def tokens_split(
    tokens,
    qkv_weight,
    conv_weight,
    decay_down,
    decay_up,
    decay_rate,
    beta_weight,
    beta_scale,
    gate_down,
    gate_up,
    norm_gain,
):
    count = tokens.shape[0]
    mixed = jnp.dot(
        tokens,
        lax.all_gather(qkv_weight, "seq", axis=1, tiled=True),
        preferred_element_type=jnp.float32,
    ).astype(jnp.bfloat16)
    earlier = from_behind(mixed[count - (CONV - 1) :], "seq", 1)
    padded = jnp.concatenate([earlier, mixed], axis=0)
    query, keys, values = features(padded, count, conv_weight)
    beta, logdec, gate_value = gates(
        tokens, decay_down, decay_up, decay_rate, beta_weight, beta_scale, gate_down, gate_up
    )
    beta_blocks = beta.reshape(count // BLOCK, BLOCK, H).transpose(0, 2, 1)
    terms = block_terms(
        to_blocks(query, count),
        to_blocks(keys, count),
        to_blocks(values, count),
        beta_blocks,
        to_blocks(logdec.reshape(count, H, DK), count),
    )
    query_up, keys_end, values_w, keys_w, attend, decay_end = terms
    identity = jnp.broadcast_to(jnp.eye(DK, dtype=jnp.float32), (H, DK, DK))
    zeroed = jnp.zeros((H, DK, DK), jnp.float32)
    (matrix, offset), unused = lax.scan(
        fold_block, (identity, zeroed), (keys_end, keys_w, values_w, decay_end)
    )

    def combine(earlier_pair, later_pair):
        return join_pairs(earlier_pair, later_pair)

    prefix = carried_in((matrix, offset), "seq", combine, (identity, zeroed))
    incoming = prefix[1]
    final_state, outputs = lax.scan(advance, incoming, terms)
    core = outputs.transpose(0, 2, 1, 3).reshape(count, H, DK)
    return finish(core, gate_value, norm_gain, count)


CHUNK = 128
NN = (((1,), (0,)), ((), ()))
NT = (((1,), (1,)), ((), ()))
TN = (((0,), (0,)), ((), ()))


def mm(a, b, dims=NN):
    return lax.dot_general(a, b, dims, preferred_element_type=jnp.float32)


def low(a):
    return a.astype(jnp.bfloat16)


def split(a):
    top = low(a)
    return top, low(a - top.astype(jnp.float32))


def mm3(a, b, dims=NN):
    (ah, al), (bh, bl) = a, b
    return mm(ah, bh, dims) + (mm(ah, bl, dims) + mm(al, bh, dims))


def product(level):
    if level == 1:
        return low, mm
    return split, mm3


LEVELS = {"g": 3, "t": 1, "s": 3, "m": 3, "c": 3}


def sigmoid(u):
    return 1.0 / (1.0 + jnp.exp(-u))


def project(rows, tok, w_at, gate_refs, mixed_s, low_s, beta_s):
    dd, gd, bw, bs = gate_refs
    width = w_at(0).shape[1]
    for t in range(3):
        got = mm(tok, w_at(t)).astype(jnp.bfloat16).astype(jnp.float32)
        mixed_s[pl.ds(pl.multiple_of(rows + 8, 8), tok.shape[0]), t * width : (t + 1) * width] = got
    low_s[pl.ds(rows, tok.shape[0]), :DK] = low(mm(tok, dd[...]))
    low_s[pl.ds(rows, tok.shape[0]), DK:] = low(mm(tok, gd[...]))
    beta_s[pl.ds(rows, tok.shape[0]), :] = bs[...] * sigmoid(mm(tok, bw[...]))


def chunk_terms(places, me, heads, refs, scratch, terms):
    conv, du, rate = refs
    mixed_s, low_s, beta_s = scratch
    m_s, b_s, p_s, q_s = terms
    C = CHUNK
    width = heads * DK
    rows = lax.broadcasted_iota(jnp.int32, (C, C), 0)
    cols = lax.broadcasted_iota(jnp.int32, (C, C), 1)
    tril = jnp.where(rows >= cols, 1.0, 0.0).astype(jnp.bfloat16)
    eye = jnp.where(rows == cols, 1.0, 0.0)
    total = conv.shape[1] // 3

    def part(t, chunk, h):
        at = pl.multiple_of(t * total + me * width + h * DK, DK)
        acc = None
        near = mixed_s[pl.ds(pl.multiple_of(chunk * C, C), C + 8), t * width + h * DK : t * width + (h + 1) * DK]
        for j in range(CONV):
            got = near[8 - (CONV - 1) + j : 8 - (CONV - 1) + j + C]
            term = conv[j : j + 1, pl.ds(at, DK)] * got
            acc = term if acc is None else acc + term
        return acc * sigmoid(acc)

    def unit(a):
        return a * lax.rsqrt(jnp.sum(a * a, axis=-1, keepdims=True) + 1e-06)

    stage = []
    for chunk, h in places:
        q = unit(part(0, chunk, h)) * DK ** (-0.5)
        k = unit(part(1, chunk, h))
        v = part(2, chunk, h)
        at = pl.multiple_of(me * width + h * DK, DK)
        down = low_s[pl.ds(pl.multiple_of(chunk * C, C), C), :DK]
        logdec = -rate[:, pl.ds(at, DK)] * sigmoid(mm(down, du[:, pl.ds(at, DK)]))
        every = beta_s[pl.ds(pl.multiple_of(chunk * C, C), C), :]
        lane = lax.broadcasted_iota(jnp.int32, every.shape, 1)
        beta = jnp.sum(jnp.where(lane == me * heads + h, every, 0.0), axis=1, keepdims=True)
        lh, ll = split(logdec)
        ls = mm(tril, lh) + mm(tril, ll)
        last = ls[C - 1 : C, :]
        grow = jnp.exp(ls)
        kup = k * grow
        stage.append((kup, k * jnp.exp(-ls), q * grow, k * jnp.exp(last - ls), v, beta, jnp.exp(last)))
    cut, dot = product(LEVELS["g"])
    lowers, attends = [], []
    for kup, kdown, qup, kend, v, beta, dec in stage:
        kd = cut(kdown)
        lowers.append(jnp.where(rows > cols, dot(cut(kup), kd, NT) * beta, 0.0))
        attends.append(jnp.where(rows >= cols, dot(cut(qup), kd, NT), 0.0))
    cut, dot = product(LEVELS["t"])
    inverse = [eye - jnp.where(rows // 2 == cols // 2, low_, 0.0) for low_ in lowers]
    size = 2
    while size < C:
        mask = jnp.logical_and(rows // (2 * size) == cols // (2 * size), rows // size != cols // size)
        ts = [cut(t) for t in inverse]
        mid = [dot(cut(jnp.where(mask, low_, 0.0)), t) for low_, t in zip(lowers, ts)]
        inverse = [t - dot(tc, cut(x)) for t, tc, x in zip(inverse, ts, mid)]
        size *= 2
    cut, dot = product(LEVELS["s"])
    solved = []
    for t, (kup, kdown, qup, kend, v, beta, dec) in zip(inverse, stage):
        tc = cut(t)
        solved.append((dot(tc, cut(v * beta)), dot(tc, cut(kup * beta))))
    cut, dot = product(LEVELS["m"])
    for (chunk, h), (vw, kw), at, (kup, kdown, qup, kend, v, beta, dec) in zip(places, solved, attends, stage):
        vc, kc, ac, ec = cut(vw), cut(kw), cut(at), cut(kend)
        slot = chunk * heads + h
        p_s[slot] = dot(ac, vc)
        q_s[slot] = qup - dot(ac, kc)
        m_s[slot] = eye * dec - dot(ec, kc, TN)
        b_s[slot] = dot(ec, vc, TN)


def run_states(chunks, me, heads, refs, low_s, terms, states, put):
    gu, gain = refs
    m_s, b_s, p_s, q_s = terms
    C = CHUNK
    width = heads * DK
    cut, dot = product(LEVELS["c"])
    for h in range(heads):
        states[h] = jnp.zeros((DK, DK), jnp.float32)

    def step(chunk, carry):
        for h in range(heads):
            slot = chunk * heads + h
            s = cut(states[h])
            core = p_s[slot] + dot(cut(q_s[slot]), s)
            states[h] = dot(cut(m_s[slot]), s) + b_s[slot]
            at = pl.multiple_of(me * width + h * DK, DK)
            gate = sigmoid(mm(low_s[pl.ds(pl.multiple_of(chunk * C, C), C), DK:], gu[:, pl.ds(at, DK)]))
            core = core * lax.rsqrt(jnp.mean(core * core, axis=-1, keepdims=True) + 1e-06) * gain[...]
            put(chunk, h, low(core * gate))
        return carry

    lax.fori_loop(0, chunks, step, 0)


def heads_kernel(n, heads, tok, w, conv, dd, du, rate, bw, bs, gd, gu, gain, out, mixed_s, low_s, beta_s, m_s, b_s, p_s, q_s, states):
    me = lax.axis_index("seq")
    count = tok.shape[0]
    chunks = count // CHUNK
    mixed_s[0:8, :] = jnp.zeros((8, mixed_s.shape[1]), jnp.float32)

    def w_at(t):
        return w[lax.rem(t * n + me, 3)]

    def first(c, carry):
        rows = pl.multiple_of(c * CHUNK, CHUNK)
        project(rows, tok[pl.ds(rows, CHUNK), :], w_at, (dd, gd, bw, bs), mixed_s, low_s, beta_s)
        return carry

    lax.fori_loop(0, chunks, first, 0)

    def second(c, carry):
        places = [(c * 2 + i, h) for i in range(2) for h in range(heads)]
        chunk_terms(places, me, heads, (conv, du, rate), (mixed_s, low_s, beta_s), (m_s, b_s, p_s, q_s))
        return carry

    lax.fori_loop(0, chunks // 2, second, 0)

    def put(chunk, h, value):
        out[pl.ds(pl.multiple_of(chunk * CHUNK, CHUNK), CHUNK), h * DK : (h + 1) * DK] = value

    run_states(chunks, me, heads, (gu, gain), low_s, (m_s, b_s, p_s, q_s), states, put)


def heads_split(tokens, qkv_weight, conv_weight, decay_down, decay_up, decay_rate, beta_weight, beta_scale, gate_down, gate_up, norm_gain):
    n, reps = lax.axis_size("seq"), lax.axis_size("rep")
    rep = lax.axis_index("rep")
    depth = qkv_weight.shape[0]
    heads = H // n
    width = heads * DK
    share = depth // reps
    everything = lax.all_gather(tokens, "seq", axis=0, tiled=True)
    mine = lax.dynamic_slice_in_dim(qkv_weight, rep * share, share, 0)
    pieces = [
        lax.ppermute(mine[:, j * width : (j + 1) * width], "seq", [(s, (3 * s + j) % n) for s in range(n)])
        for j in range(3)
    ]
    weight = lax.all_gather(jnp.stack(pieces), "rep", axis=1, tiled=True)
    count = everything.shape[0]
    slots = count // CHUNK * heads
    square = pltpu.VMEM((slots, DK, DK), jnp.float32)
    attended = pl.pallas_call(
        functools.partial(heads_kernel, n, heads),
        out_shape=jax.ShapeDtypeStruct((count, width), jnp.bfloat16),
        in_specs=[pl.BlockSpec(memory_space=pltpu.VMEM)] * 11,
        out_specs=pl.BlockSpec(memory_space=pltpu.VMEM),
        scratch_shapes=[
            pltpu.VMEM((count + 8, 3 * width), jnp.float32),
            pltpu.VMEM((count, 2 * DK), jnp.bfloat16),
            pltpu.VMEM((count, H), jnp.float32),
            square, square, square, square,
            pltpu.VMEM((heads, DK, DK), jnp.float32),
        ],
        compiler_params=pltpu.CompilerParams(vmem_limit_bytes=48 * 2**20),
    )(everything, weight, conv_weight, decay_down, decay_up, decay_rate.reshape(1, -1), beta_weight, beta_scale.reshape(1, -1), gate_down, gate_up, norm_gain.reshape(1, -1))
    return lax.all_to_all(attended, "seq", 0, 1, tiled=True)


def by_heads(mesh):
    n, reps = mesh.shape["seq"], mesh.shape["rep"]
    return H % n == 0 and n % 3 != 0


def solution(mesh):
    in_specs = (
        P(("rep", "seq"), None),
        P(None, "seq"),
        P(),
        P(),
        P(),
        P(),
        P(),
        P(),
        P(),
        P(),
        P(),
    )
    out_specs = P(("rep", "seq"), None)
    return jax.shard_map(
        heads_split if by_heads(mesh) else tokens_split, mesh=mesh, in_specs=in_specs, out_specs=out_specs, check_vma=False
    )
```

```python
import functools
import jax
import jax.numpy as jnp
from jax import lax
from jax.experimental import pallas as pl
from jax.experimental.pallas import tpu as pltpu
from jax.sharding import PartitionSpec as P

H = 16
DK = 128
CONV = 4
BLOCK = 64


precise = lax.Precision.HIGHEST


def from_behind(block, axis, distance):
    devices = range(lax.axis_size(axis))
    route = [(i - distance, i) for i in devices if i - distance in devices]
    return lax.ppermute(block, axis, route)


def carried_in(x, axis, combine, identity):
    devices, mine = (lax.axis_size(axis), lax.axis_index(axis))
    everything = jax.tree.map(lambda part: lax.all_gather(part, axis), x)
    start = jax.tree.map(
        lambda part, zero: jnp.broadcast_to(jnp.asarray(zero, part.dtype), part.shape), x, identity
    )

    def lap(k, before):
        reached = k < mine
        new = combine(before, jax.tree.map(lambda part: part[k], everything))
        return jax.tree.map(lambda a, b: jnp.where(reached, a, b), new, before)

    return lax.fori_loop(0, devices, lap, start)


def unit_rows(vector):
    return vector * lax.rsqrt(jnp.sum(vector * vector, axis=-1, keepdims=True) + 1e-06)


def features(padded, count, conv_weight):
    combined = conv_weight[0] * padded[0:count].astype(jnp.float32)
    for offset in range(1, CONV):
        combined = combined + conv_weight[offset] * padded[offset : offset + count].astype(
            jnp.float32
        )
    active = jax.nn.silu(combined).reshape(count, 3, H, DK)
    query = unit_rows(active[:, 0]) * DK ** (-0.5)
    keys = unit_rows(active[:, 1])
    values = active[:, 2]
    return (query, keys, values)


def gates(tokens, decay_down, decay_up, decay_rate, beta_weight, beta_scale, gate_down, gate_up):
    beta = beta_scale * jax.nn.sigmoid(
        jnp.dot(tokens, beta_weight, preferred_element_type=jnp.float32)
    )
    decay_low = jnp.dot(tokens, decay_down, preferred_element_type=jnp.float32).astype(jnp.bfloat16)
    logdec = -decay_rate * jax.nn.sigmoid(
        jnp.dot(decay_low, decay_up, preferred_element_type=jnp.float32)
    )
    gate_low = jnp.dot(tokens, gate_down, preferred_element_type=jnp.float32).astype(jnp.bfloat16)
    gate_value = jax.nn.sigmoid(jnp.dot(gate_low, gate_up, preferred_element_type=jnp.float32))
    return (beta, logdec, gate_value)


def to_blocks(array, count):
    return array.reshape(count // BLOCK, BLOCK, H, array.shape[-1]).transpose(0, 2, 1, 3)


def block_terms(query, keys, values, beta, logdec):
    log_sum = jnp.cumsum(logdec, axis=2)
    grow = jnp.exp(log_sum)
    keys_up = keys * grow
    keys_down = keys * jnp.exp(-log_sum)
    query_up = query * grow
    keys_end = keys * jnp.exp(log_sum[:, :, -1:, :] - log_sum)
    length = query.shape[2]
    rows = lax.broadcasted_iota(jnp.int32, (length, length), 0)
    columns = lax.broadcasted_iota(jnp.int32, (length, length), 1)
    scores = jnp.einsum("nhic,nhjc->nhij", keys_up, keys_down, precision=precise) * beta[..., None]
    system = jnp.where(rows > columns, scores, 0.0) + jnp.eye(length, dtype=jnp.float32)
    right_side = jnp.concatenate([values, keys_up], axis=-1) * beta[..., None]
    solved = jax.scipy.linalg.solve_triangular(system, right_side, lower=True, unit_diagonal=True)
    values_w = solved[..., :DK]
    keys_w = solved[..., DK:]
    attend = jnp.where(
        rows >= columns, jnp.einsum("nhic,nhjc->nhij", query_up, keys_down, precision=precise), 0.0
    )
    decay_end = jnp.exp(log_sum[:, :, -1, :])
    return (query_up, keys_end, values_w, keys_w, attend, decay_end)


def advance(state, inputs):
    query_up, keys_end, values_w, keys_w, attend, decay_end = inputs
    update = values_w - jnp.einsum("hcd,hde->hce", keys_w, state, precision=precise)
    output = jnp.einsum("hcd,hde->hce", query_up, state, precision=precise)
    output = output + jnp.einsum("hij,hje->hie", attend, update, precision=precise)
    state = decay_end[..., None] * state + jnp.einsum(
        "hcd,hce->hde", keys_end, update, precision=precise
    )
    return (state, output)


def matmul(left, right):
    return jnp.einsum("...de,...ef->...df", left, right, precision=precise)


def fold_block(carry, inputs):
    matrix, offset = carry
    keys_end, keys_w, values_w, decay_end = inputs
    eye_block = jnp.eye(DK, dtype=jnp.float32)
    block_matrix = decay_end[..., None] * eye_block - jnp.einsum(
        "hcd,hce->hde", keys_end, keys_w, precision=precise
    )
    block_offset = jnp.einsum("hcd,hce->hde", keys_end, values_w, precision=precise)
    return ((matmul(block_matrix, matrix), matmul(block_matrix, offset) + block_offset), None)


def join_pairs(first, second):
    return (matmul(second[0], first[0]), matmul(second[0], first[1]) + second[1])


def finish(core, gate_value, norm_gain, count):
    scaled = core * lax.rsqrt(jnp.mean(core * core, axis=-1, keepdims=True) + 1e-06) * norm_gain
    return (scaled.reshape(count, H * DK) * gate_value).astype(jnp.bfloat16)


def tokens_split(
    tokens,
    qkv_weight,
    conv_weight,
    decay_down,
    decay_up,
    decay_rate,
    beta_weight,
    beta_scale,
    gate_down,
    gate_up,
    norm_gain,
):
    count = tokens.shape[0]
    mixed = jnp.dot(
        tokens,
        lax.all_gather(qkv_weight, "seq", axis=1, tiled=True),
        preferred_element_type=jnp.float32,
    ).astype(jnp.bfloat16)
    earlier = from_behind(mixed[count - (CONV - 1) :], "seq", 1)
    padded = jnp.concatenate([earlier, mixed], axis=0)
    query, keys, values = features(padded, count, conv_weight)
    beta, logdec, gate_value = gates(
        tokens, decay_down, decay_up, decay_rate, beta_weight, beta_scale, gate_down, gate_up
    )
    beta_blocks = beta.reshape(count // BLOCK, BLOCK, H).transpose(0, 2, 1)
    terms = block_terms(
        to_blocks(query, count),
        to_blocks(keys, count),
        to_blocks(values, count),
        beta_blocks,
        to_blocks(logdec.reshape(count, H, DK), count),
    )
    query_up, keys_end, values_w, keys_w, attend, decay_end = terms
    identity = jnp.broadcast_to(jnp.eye(DK, dtype=jnp.float32), (H, DK, DK))
    zeroed = jnp.zeros((H, DK, DK), jnp.float32)
    (matrix, offset), unused = lax.scan(
        fold_block, (identity, zeroed), (keys_end, keys_w, values_w, decay_end)
    )

    def combine(earlier_pair, later_pair):
        return join_pairs(earlier_pair, later_pair)

    prefix = carried_in((matrix, offset), "seq", combine, (identity, zeroed))
    incoming = prefix[1]
    final_state, outputs = lax.scan(advance, incoming, terms)
    core = outputs.transpose(0, 2, 1, 3).reshape(count, H, DK)
    return finish(core, gate_value, norm_gain, count)


CHUNK = 128
NN = (((1,), (0,)), ((), ()))
NT = (((1,), (1,)), ((), ()))
TN = (((0,), (0,)), ((), ()))


def mm(a, b, dims=NN):
    return lax.dot_general(a, b, dims, preferred_element_type=jnp.float32)


def low(a):
    return a.astype(jnp.bfloat16)


def split(a):
    top = low(a)
    return top, low(a - top.astype(jnp.float32))


def mm3(a, b, dims=NN):
    (ah, al), (bh, bl) = a, b
    return mm(ah, bh, dims) + (mm(ah, bl, dims) + mm(al, bh, dims))


def product(level):
    if level == 1:
        return low, mm
    return split, mm3


LEVELS = {"g": 3, "t": 1, "s": 3, "m": 3, "c": 3}


def sigmoid(u):
    return 1.0 / (1.0 + jnp.exp(-u))


def project(rows, tok, w_at, gate_refs, mixed_s, low_s, beta_s):
    dd, gd, bw, bs = gate_refs
    width = w_at(0).shape[1]
    for t in range(3):
        got = mm(tok, w_at(t)).astype(jnp.bfloat16).astype(jnp.float32)
        mixed_s[pl.ds(pl.multiple_of(rows + 8, 8), tok.shape[0]), t * width : (t + 1) * width] = got
    low_s[pl.ds(rows, tok.shape[0]), :DK] = low(mm(tok, dd[...]))
    low_s[pl.ds(rows, tok.shape[0]), DK:] = low(mm(tok, gd[...]))
    beta_s[pl.ds(rows, tok.shape[0]), :] = bs[...] * sigmoid(mm(tok, bw[...]))


def chunk_terms(places, me, heads, refs, scratch, terms):
    conv, du, rate = refs
    mixed_s, low_s, beta_s = scratch
    m_s, b_s, p_s, q_s = terms
    C = CHUNK
    width = heads * DK
    rows = lax.broadcasted_iota(jnp.int32, (C, C), 0)
    cols = lax.broadcasted_iota(jnp.int32, (C, C), 1)
    tril = jnp.where(rows >= cols, 1.0, 0.0).astype(jnp.bfloat16)
    eye = jnp.where(rows == cols, 1.0, 0.0)
    total = conv.shape[1] // 3

    def part(t, chunk, h):
        at = pl.multiple_of(t * total + me * width + h * DK, DK)
        acc = None
        near = mixed_s[pl.ds(pl.multiple_of(chunk * C, C), C + 8), t * width + h * DK : t * width + (h + 1) * DK]
        for j in range(CONV):
            got = near[8 - (CONV - 1) + j : 8 - (CONV - 1) + j + C]
            term = conv[j : j + 1, pl.ds(at, DK)] * got
            acc = term if acc is None else acc + term
        return acc * sigmoid(acc)

    def unit(a):
        return a * lax.rsqrt(jnp.sum(a * a, axis=-1, keepdims=True) + 1e-06)

    stage = []
    for chunk, h in places:
        q = unit(part(0, chunk, h)) * DK ** (-0.5)
        k = unit(part(1, chunk, h))
        v = part(2, chunk, h)
        at = pl.multiple_of(me * width + h * DK, DK)
        down = low_s[pl.ds(pl.multiple_of(chunk * C, C), C), :DK]
        logdec = -rate[:, pl.ds(at, DK)] * sigmoid(mm(down, du[:, pl.ds(at, DK)]))
        every = beta_s[pl.ds(pl.multiple_of(chunk * C, C), C), :]
        lane = lax.broadcasted_iota(jnp.int32, every.shape, 1)
        beta = jnp.sum(jnp.where(lane == me * heads + h, every, 0.0), axis=1, keepdims=True)
        lh, ll = split(logdec)
        ls = mm(tril, lh) + mm(tril, ll)
        last = ls[C - 1 : C, :]
        grow = jnp.exp(ls)
        kup = k * grow
        stage.append((kup, k * jnp.exp(-ls), q * grow, k * jnp.exp(last - ls), v, beta, jnp.exp(last)))
    cut, dot = product(LEVELS["g"])
    lowers, attends = [], []
    for kup, kdown, qup, kend, v, beta, dec in stage:
        kd = cut(kdown)
        lowers.append(jnp.where(rows > cols, dot(cut(kup), kd, NT) * beta, 0.0))
        attends.append(jnp.where(rows >= cols, dot(cut(qup), kd, NT), 0.0))
    cut, dot = product(LEVELS["t"])
    inverse = [eye - jnp.where(rows // 2 == cols // 2, low_, 0.0) for low_ in lowers]
    size = 2
    while size < C:
        mask = jnp.logical_and(rows // (2 * size) == cols // (2 * size), rows // size != cols // size)
        ts = [cut(t) for t in inverse]
        mid = [dot(cut(jnp.where(mask, low_, 0.0)), t) for low_, t in zip(lowers, ts)]
        inverse = [t - dot(tc, cut(x)) for t, tc, x in zip(inverse, ts, mid)]
        size *= 2
    cut, dot = product(LEVELS["s"])
    solved = []
    for t, (kup, kdown, qup, kend, v, beta, dec) in zip(inverse, stage):
        tc = cut(t)
        solved.append((dot(tc, cut(v * beta)), dot(tc, cut(kup * beta))))
    cut, dot = product(LEVELS["m"])
    for (chunk, h), (vw, kw), at, (kup, kdown, qup, kend, v, beta, dec) in zip(places, solved, attends, stage):
        vc, kc, ac, ec = cut(vw), cut(kw), cut(at), cut(kend)
        slot = chunk * heads + h
        p_s[slot] = dot(ac, vc)
        q_s[slot] = qup - dot(ac, kc)
        m_s[slot] = eye * dec - dot(ec, kc, TN)
        b_s[slot] = dot(ec, vc, TN)


def run_states(chunks, me, heads, refs, low_s, terms, states, put):
    gu, gain = refs
    m_s, b_s, p_s, q_s = terms
    C = CHUNK
    width = heads * DK
    cut, dot = product(LEVELS["c"])
    for h in range(heads):
        states[h] = jnp.zeros((DK, DK), jnp.float32)

    def step(chunk, carry):
        for h in range(heads):
            slot = chunk * heads + h
            s = cut(states[h])
            core = p_s[slot] + dot(cut(q_s[slot]), s)
            states[h] = dot(cut(m_s[slot]), s) + b_s[slot]
            at = pl.multiple_of(me * width + h * DK, DK)
            gate = sigmoid(mm(low_s[pl.ds(pl.multiple_of(chunk * C, C), C), DK:], gu[:, pl.ds(at, DK)]))
            core = core * lax.rsqrt(jnp.mean(core * core, axis=-1, keepdims=True) + 1e-06) * gain[...]
            put(chunk, h, low(core * gate))
        return carry

    lax.fori_loop(0, chunks, step, 0)


MESH = pl.DeviceIdType.MESH


def ring_place(device, n):
    return jnp.where(device % 2 == 0, device // 2, n - 1 - device // 2)


def ring_device(place, n):
    return jnp.where(place < n // 2, 2 * place, 2 * (n - 1 - place) + 1)


def greet(n):
    me, rep = lax.axis_index("seq"), lax.axis_index("rep")
    barrier = pltpu.get_barrier_semaphore()
    for k in range(1, n):
        pl.semaphore_signal(barrier, inc=1, device_id={"seq": (me + k) % n}, device_id_type=MESH)
    for other in ((rep + 2) % 4, rep + 1 - 2 * (rep % 2)):
        pl.semaphore_signal(barrier, inc=1, device_id={"rep": other}, device_id_type=MESH)
    pl.semaphore_wait(barrier, n + 1)


def remote(src, dst, sems, k, to):
    return pltpu.make_async_remote_copy(
        src_ref=src, dst_ref=dst, send_sem=sems[0].at[k], recv_sem=sems[1].at[k], device_id=to, device_id_type=MESH
    )


def ring_copies(n, blocks, sems):
    me = lax.axis_index("seq")
    place = ring_place(me, n)
    right = {"seq": ring_device((place + 1) % n, n)}
    left = {"seq": ring_device((place + n - 1) % n, n)}
    half = blocks.shape[1] // 2
    steps = []
    for k in range(n // 2):
        goes_right = blocks.at[ring_device((place + n - k) % n, n)]
        goes_left = blocks.at[ring_device((place + k) % n, n)]
        comes_left = blocks.at[ring_device((place + n - k - 1) % n, n)]
        comes_right = blocks.at[ring_device((place + k + 1) % n, n)]
        if k == n // 2 - 1:
            goes_right, comes_left = goes_right.at[pl.ds(0, half)], comes_left.at[pl.ds(0, half)]
            goes_left, comes_right = goes_left.at[pl.ds(half, half)], comes_right.at[pl.ds(half, half)]
        steps.append(
            (
                remote(goes_right, goes_right, sems, 2 * k, right),
                remote(goes_left, goes_left, sems, 2 * k + 1, left),
                remote(comes_left, comes_left, sems, 2 * k, left),
                remote(comes_right, comes_right, sems, 2 * k + 1, right),
            )
        )
    return steps


class WeightMoves:
    def __init__(self, n, source, held, sems, local_sems):
        self.n, self.held = n, held
        me, rep = lax.axis_index("seq"), lax.axis_index("rep")
        width = held.shape[2]
        share = held.shape[1] // 4
        inverse = pow(3, -1, n)
        across, beside = (rep + 2) % 4, rep + 1 - 2 * (rep % 2)
        rows = lambda r: pl.ds(pl.multiple_of(r * share, 16), share)
        self.out, self.sent_here, self.came_here, self.local = [], [], [], []
        self.to_across, self.to_beside, self.onward = [], [], []
        self.from_across, self.from_beside, self.from_onward = [], [], []
        for j in range(3):
            piece = source.at[rows(rep), j * width : (j + 1) * width]
            mine = held.at[j, rows(rep)]
            to = (3 * me + j) % n
            self.sent_here.append(to == me)
            self.came_here.append((inverse * (me + n - j)) % n == me)
            self.out.append(remote(piece, mine, sems, j, {"seq": to}))
            self.local.append(pltpu.make_async_copy(piece, mine, local_sems.at[j]))
            self.to_across.append(remote(mine, mine, sems, 3 + j, {"rep": across}))
            self.to_beside.append(remote(mine, mine, sems, 6 + j, {"rep": beside}))
            over = held.at[j, rows(across)]
            self.from_across.append(remote(over, over, sems, 3 + j, {"rep": across}))
            self.onward.append(remote(over, over, sems, 9 + j, {"rep": beside}))
            near = held.at[j, rows(beside)]
            self.from_beside.append(remote(near, near, sems, 6 + j, {"rep": beside}))
            far = held.at[j, rows((beside + 2) % 4)]
            self.from_onward.append(remote(far, far, sems, 9 + j, {"rep": beside}))

    def begin(self):
        for j in range(3):
            pl.when(self.sent_here[j])(self.local[j].start)
            pl.when(jnp.logical_not(self.sent_here[j]))(self.out[j].start)

    def spread(self):
        for j in range(3):
            pl.when(self.came_here[j])(self.local[j].wait)
            pl.when(jnp.logical_not(self.came_here[j]))(self.out[j].wait_recv)
            self.to_across[j].start()
            self.to_beside[j].start()

    def pass_on(self):
        for j in range(3):
            self.from_across[j].wait_recv()
            self.onward[j].start()

    def finish(self):
        for j in range(3):
            self.from_beside[j].wait_recv()
            self.from_onward[j].wait_recv()

    def sent(self):
        for j in range(3):
            pl.when(jnp.logical_not(self.sent_here[j]))(self.out[j].wait_send)
            self.to_across[j].wait_send()
            self.to_beside[j].wait_send()
            self.onward[j].wait_send()


def gather_kernel(n, tok, w, blocks, held, tok_send, tok_recv, w_send, w_recv, local):
    me = lax.axis_index("seq")
    own = pltpu.make_async_copy(tok, blocks.at[me], local.at[3])
    own.start()
    greet(n)
    moves = WeightMoves(n, w, held, (w_send, w_recv), local)
    moves.begin()
    own.wait()
    steps = ring_copies(n, blocks, (tok_send, tok_recv))
    for k, (right, left, came_left, came_right) in enumerate(steps):
        right.start()
        left.start()
        if k == 0:
            moves.spread()
        if k == 1:
            moves.pass_on()
        came_left.wait_recv()
        came_right.wait_recv()
    moves.finish()
    moves.sent()
    for right, left, came_left, came_right in steps:
        right.wait_send()
        left.wait_send()


def gathered(tokens, qkv_weight, n, width):
    depth = qkv_weight.shape[0]
    anywhere = pl.BlockSpec(memory_space=pl.ANY)
    return pl.pallas_call(
        functools.partial(gather_kernel, n),
        out_shape=[
            jax.ShapeDtypeStruct((n,) + tokens.shape, tokens.dtype),
            jax.ShapeDtypeStruct((3, depth, width), qkv_weight.dtype),
        ],
        in_specs=[anywhere] * 2,
        out_specs=[anywhere] * 2,
        scratch_shapes=[
            pltpu.SemaphoreType.DMA((n,)),
            pltpu.SemaphoreType.DMA((n,)),
            pltpu.SemaphoreType.DMA((12,)),
            pltpu.SemaphoreType.DMA((12,)),
            pltpu.SemaphoreType.DMA((4,)),
        ],
        compiler_params=pltpu.CompilerParams(collective_id=0, has_side_effects=True),
    )(tokens, qkv_weight)


def heads_kernel(n, heads, tok, w, conv, dd, du, rate, bw, bs, gd, gu, gain, out, mixed_s, low_s, beta_s, m_s, b_s, p_s, q_s, states):
    me = lax.axis_index("seq")
    count = tok.shape[0]
    chunks = count // CHUNK
    mixed_s[0:8, :] = jnp.zeros((8, mixed_s.shape[1]), jnp.float32)

    def w_at(t):
        return w[lax.rem(t * n + me, 3)]

    def first(c, carry):
        rows = pl.multiple_of(c * CHUNK, CHUNK)
        project(rows, tok[pl.ds(rows, CHUNK), :], w_at, (dd, gd, bw, bs), mixed_s, low_s, beta_s)
        return carry

    lax.fori_loop(0, chunks, first, 0)

    def second(c, carry):
        places = [(c * 2 + i, h) for i in range(2) for h in range(heads)]
        chunk_terms(places, me, heads, (conv, du, rate), (mixed_s, low_s, beta_s), (m_s, b_s, p_s, q_s))
        return carry

    lax.fori_loop(0, chunks // 2, second, 0)

    def put(chunk, h, value):
        out[pl.ds(pl.multiple_of(chunk * CHUNK, CHUNK), CHUNK), h * DK : (h + 1) * DK] = value

    run_states(chunks, me, heads, (gu, gain), low_s, (m_s, b_s, p_s, q_s), states, put)


def heads_split(tokens, qkv_weight, conv_weight, decay_down, decay_up, decay_rate, beta_weight, beta_scale, gate_down, gate_up, norm_gain):
    n = lax.axis_size("seq")
    heads = H // n
    width = heads * DK
    blocks, weight = gathered(tokens, qkv_weight, n, width)
    everything = blocks.reshape(-1, tokens.shape[1])
    count = everything.shape[0]
    slots = count // CHUNK * heads
    square = pltpu.VMEM((slots, DK, DK), jnp.float32)
    attended = pl.pallas_call(
        functools.partial(heads_kernel, n, heads),
        out_shape=jax.ShapeDtypeStruct((count, width), jnp.bfloat16),
        in_specs=[pl.BlockSpec(memory_space=pltpu.VMEM)] * 11,
        out_specs=pl.BlockSpec(memory_space=pltpu.VMEM),
        scratch_shapes=[
            pltpu.VMEM((count + 8, 3 * width), jnp.float32),
            pltpu.VMEM((count, 2 * DK), jnp.bfloat16),
            pltpu.VMEM((count, H), jnp.float32),
            square, square, square, square,
            pltpu.VMEM((heads, DK, DK), jnp.float32),
        ],
        compiler_params=pltpu.CompilerParams(vmem_limit_bytes=48 * 2**20),
    )(everything, weight, conv_weight, decay_down, decay_up, decay_rate.reshape(1, -1), beta_weight, beta_scale.reshape(1, -1), gate_down, gate_up, norm_gain.reshape(1, -1))
    return lax.all_to_all(attended, "seq", 0, 1, tiled=True)


def by_heads(mesh):
    n, reps = mesh.shape["seq"], mesh.shape["rep"]
    return H % n == 0 and n % 3 != 0 and n % 2 == 0 and reps == 4


def solution(mesh):
    in_specs = (
        P(("rep", "seq"), None),
        P(None, "seq"),
        P(),
        P(),
        P(),
        P(),
        P(),
        P(),
        P(),
        P(),
        P(),
    )
    out_specs = P(("rep", "seq"), None)
    return jax.shard_map(
        heads_split if by_heads(mesh) else tokens_split, mesh=mesh, in_specs=in_specs, out_specs=out_specs, check_vma=False
    )
```

```python
import functools
import jax
import jax.numpy as jnp
from jax import lax
from jax.experimental import pallas as pl
from jax.experimental.pallas import tpu as pltpu
from jax.sharding import PartitionSpec as P

H = 16
DK = 128
CONV = 4
BLOCK = 64


precise = lax.Precision.HIGHEST


def from_behind(block, axis, distance):
    devices = range(lax.axis_size(axis))
    route = [(i - distance, i) for i in devices if i - distance in devices]
    return lax.ppermute(block, axis, route)


def carried_in(x, axis, combine, identity):
    devices, mine = (lax.axis_size(axis), lax.axis_index(axis))
    everything = jax.tree.map(lambda part: lax.all_gather(part, axis), x)
    start = jax.tree.map(
        lambda part, zero: jnp.broadcast_to(jnp.asarray(zero, part.dtype), part.shape), x, identity
    )

    def lap(k, before):
        reached = k < mine
        new = combine(before, jax.tree.map(lambda part: part[k], everything))
        return jax.tree.map(lambda a, b: jnp.where(reached, a, b), new, before)

    return lax.fori_loop(0, devices, lap, start)


def unit_rows(vector):
    return vector * lax.rsqrt(jnp.sum(vector * vector, axis=-1, keepdims=True) + 1e-06)


def features(padded, count, conv_weight):
    combined = conv_weight[0] * padded[0:count].astype(jnp.float32)
    for offset in range(1, CONV):
        combined = combined + conv_weight[offset] * padded[offset : offset + count].astype(
            jnp.float32
        )
    active = jax.nn.silu(combined).reshape(count, 3, H, DK)
    query = unit_rows(active[:, 0]) * DK ** (-0.5)
    keys = unit_rows(active[:, 1])
    values = active[:, 2]
    return (query, keys, values)


def gates(tokens, decay_down, decay_up, decay_rate, beta_weight, beta_scale, gate_down, gate_up):
    beta = beta_scale * jax.nn.sigmoid(
        jnp.dot(tokens, beta_weight, preferred_element_type=jnp.float32)
    )
    decay_low = jnp.dot(tokens, decay_down, preferred_element_type=jnp.float32).astype(jnp.bfloat16)
    logdec = -decay_rate * jax.nn.sigmoid(
        jnp.dot(decay_low, decay_up, preferred_element_type=jnp.float32)
    )
    gate_low = jnp.dot(tokens, gate_down, preferred_element_type=jnp.float32).astype(jnp.bfloat16)
    gate_value = jax.nn.sigmoid(jnp.dot(gate_low, gate_up, preferred_element_type=jnp.float32))
    return (beta, logdec, gate_value)


def to_blocks(array, count):
    return array.reshape(count // BLOCK, BLOCK, H, array.shape[-1]).transpose(0, 2, 1, 3)


def block_terms(query, keys, values, beta, logdec):
    log_sum = jnp.cumsum(logdec, axis=2)
    grow = jnp.exp(log_sum)
    keys_up = keys * grow
    keys_down = keys * jnp.exp(-log_sum)
    query_up = query * grow
    keys_end = keys * jnp.exp(log_sum[:, :, -1:, :] - log_sum)
    length = query.shape[2]
    rows = lax.broadcasted_iota(jnp.int32, (length, length), 0)
    columns = lax.broadcasted_iota(jnp.int32, (length, length), 1)
    scores = jnp.einsum("nhic,nhjc->nhij", keys_up, keys_down, precision=precise) * beta[..., None]
    system = jnp.where(rows > columns, scores, 0.0) + jnp.eye(length, dtype=jnp.float32)
    right_side = jnp.concatenate([values, keys_up], axis=-1) * beta[..., None]
    solved = jax.scipy.linalg.solve_triangular(system, right_side, lower=True, unit_diagonal=True)
    values_w = solved[..., :DK]
    keys_w = solved[..., DK:]
    attend = jnp.where(
        rows >= columns, jnp.einsum("nhic,nhjc->nhij", query_up, keys_down, precision=precise), 0.0
    )
    decay_end = jnp.exp(log_sum[:, :, -1, :])
    return (query_up, keys_end, values_w, keys_w, attend, decay_end)


def advance(state, inputs):
    query_up, keys_end, values_w, keys_w, attend, decay_end = inputs
    update = values_w - jnp.einsum("hcd,hde->hce", keys_w, state, precision=precise)
    output = jnp.einsum("hcd,hde->hce", query_up, state, precision=precise)
    output = output + jnp.einsum("hij,hje->hie", attend, update, precision=precise)
    state = decay_end[..., None] * state + jnp.einsum(
        "hcd,hce->hde", keys_end, update, precision=precise
    )
    return (state, output)


def matmul(left, right):
    return jnp.einsum("...de,...ef->...df", left, right, precision=precise)


def fold_block(carry, inputs):
    matrix, offset = carry
    keys_end, keys_w, values_w, decay_end = inputs
    eye_block = jnp.eye(DK, dtype=jnp.float32)
    block_matrix = decay_end[..., None] * eye_block - jnp.einsum(
        "hcd,hce->hde", keys_end, keys_w, precision=precise
    )
    block_offset = jnp.einsum("hcd,hce->hde", keys_end, values_w, precision=precise)
    return ((matmul(block_matrix, matrix), matmul(block_matrix, offset) + block_offset), None)


def join_pairs(first, second):
    return (matmul(second[0], first[0]), matmul(second[0], first[1]) + second[1])


def finish(core, gate_value, norm_gain, count):
    scaled = core * lax.rsqrt(jnp.mean(core * core, axis=-1, keepdims=True) + 1e-06) * norm_gain
    return (scaled.reshape(count, H * DK) * gate_value).astype(jnp.bfloat16)


def tokens_split(
    tokens,
    qkv_weight,
    conv_weight,
    decay_down,
    decay_up,
    decay_rate,
    beta_weight,
    beta_scale,
    gate_down,
    gate_up,
    norm_gain,
):
    count = tokens.shape[0]
    mixed = jnp.dot(
        tokens,
        lax.all_gather(qkv_weight, "seq", axis=1, tiled=True),
        preferred_element_type=jnp.float32,
    ).astype(jnp.bfloat16)
    earlier = from_behind(mixed[count - (CONV - 1) :], "seq", 1)
    padded = jnp.concatenate([earlier, mixed], axis=0)
    query, keys, values = features(padded, count, conv_weight)
    beta, logdec, gate_value = gates(
        tokens, decay_down, decay_up, decay_rate, beta_weight, beta_scale, gate_down, gate_up
    )
    beta_blocks = beta.reshape(count // BLOCK, BLOCK, H).transpose(0, 2, 1)
    terms = block_terms(
        to_blocks(query, count),
        to_blocks(keys, count),
        to_blocks(values, count),
        beta_blocks,
        to_blocks(logdec.reshape(count, H, DK), count),
    )
    query_up, keys_end, values_w, keys_w, attend, decay_end = terms
    identity = jnp.broadcast_to(jnp.eye(DK, dtype=jnp.float32), (H, DK, DK))
    zeroed = jnp.zeros((H, DK, DK), jnp.float32)
    (matrix, offset), unused = lax.scan(
        fold_block, (identity, zeroed), (keys_end, keys_w, values_w, decay_end)
    )

    def combine(earlier_pair, later_pair):
        return join_pairs(earlier_pair, later_pair)

    prefix = carried_in((matrix, offset), "seq", combine, (identity, zeroed))
    incoming = prefix[1]
    final_state, outputs = lax.scan(advance, incoming, terms)
    core = outputs.transpose(0, 2, 1, 3).reshape(count, H, DK)
    return finish(core, gate_value, norm_gain, count)


CHUNK = 128
NN = (((1,), (0,)), ((), ()))
NT = (((1,), (1,)), ((), ()))
TN = (((0,), (0,)), ((), ()))


def mm(a, b, dims=NN):
    return lax.dot_general(a, b, dims, preferred_element_type=jnp.float32)


def low(a):
    return a.astype(jnp.bfloat16)


def split(a):
    top = low(a)
    return top, low(a - top.astype(jnp.float32))


def mm3(a, b, dims=NN):
    (ah, al), (bh, bl) = a, b
    return mm(ah, bh, dims) + (mm(ah, bl, dims) + mm(al, bh, dims))


def product(level):
    if level == 1:
        return low, mm
    return split, mm3


LEVELS = {"g": 1, "t": 1, "s": 1, "m": 3, "c": 3}


def sigmoid(u):
    return 1.0 / (1.0 + jnp.exp(-u))


def project(rows, tok, w_at, gate_refs, mixed_s, low_s, beta_s):
    dd, gd, bw, bs = gate_refs
    width = w_at(0).shape[1]
    for t in range(3):
        got = mm(tok, w_at(t)).astype(jnp.bfloat16).astype(jnp.float32)
        mixed_s[pl.ds(pl.multiple_of(rows + 8, 8), tok.shape[0]), t * width : (t + 1) * width] = got
    low_s[pl.ds(rows, tok.shape[0]), :DK] = low(mm(tok, dd[...]))
    low_s[pl.ds(rows, tok.shape[0]), DK:] = low(mm(tok, gd[...]))
    beta_s[pl.ds(rows, tok.shape[0]), :] = bs[...] * sigmoid(mm(tok, bw[...]))


def chunk_terms(places, me, heads, refs, scratch, terms):
    conv, du, rate = refs
    mixed_s, low_s, beta_s = scratch
    m_s, b_s, p_s, q_s = terms
    C = CHUNK
    width = heads * DK
    rows = lax.broadcasted_iota(jnp.int32, (C, C), 0)
    cols = lax.broadcasted_iota(jnp.int32, (C, C), 1)
    tril = jnp.where(rows >= cols, 1.0, 0.0).astype(jnp.bfloat16)
    eye = jnp.where(rows == cols, 1.0, 0.0)
    total = conv.shape[1] // 3

    def part(t, chunk, h):
        at = pl.multiple_of(t * total + me * width + h * DK, DK)
        acc = None
        near = mixed_s[pl.ds(pl.multiple_of(chunk * C, C), C + 8), t * width + h * DK : t * width + (h + 1) * DK]
        for j in range(CONV):
            got = near[8 - (CONV - 1) + j : 8 - (CONV - 1) + j + C]
            term = conv[j : j + 1, pl.ds(at, DK)] * got
            acc = term if acc is None else acc + term
        return acc * sigmoid(acc)

    def unit(a):
        return a * lax.rsqrt(jnp.sum(a * a, axis=-1, keepdims=True) + 1e-06)

    stage = []
    for chunk, h in places:
        q = unit(part(0, chunk, h)) * DK ** (-0.5)
        k = unit(part(1, chunk, h))
        v = part(2, chunk, h)
        at = pl.multiple_of(me * width + h * DK, DK)
        down = low_s[pl.ds(pl.multiple_of(chunk * C, C), C), :DK]
        logdec = -rate[:, pl.ds(at, DK)] * sigmoid(mm(down, du[:, pl.ds(at, DK)]))
        every = beta_s[pl.ds(pl.multiple_of(chunk * C, C), C), :]
        lane = lax.broadcasted_iota(jnp.int32, every.shape, 1)
        beta = jnp.sum(jnp.where(lane == me * heads + h, every, 0.0), axis=1, keepdims=True)
        lh, ll = split(logdec)
        ls = mm(tril, lh) + mm(tril, ll)
        last = ls[C - 1 : C, :]
        grow = jnp.exp(ls)
        kup = k * grow
        stage.append((kup, k * jnp.exp(-ls), q * grow, k * jnp.exp(last - ls), v, beta, jnp.exp(last)))
    cut, dot = product(LEVELS["g"])
    lowers, attends = [], []
    for kup, kdown, qup, kend, v, beta, dec in stage:
        kd = cut(kdown)
        lowers.append(jnp.where(rows > cols, dot(cut(kup), kd, NT) * beta, 0.0))
        attends.append(jnp.where(rows >= cols, dot(cut(qup), kd, NT), 0.0))
    cut, dot = product(LEVELS["t"])
    inverse = [eye - jnp.where(rows // 2 == cols // 2, low_, 0.0) for low_ in lowers]
    size = 2
    while size < C:
        mask = jnp.logical_and(rows // (2 * size) == cols // (2 * size), rows // size != cols // size)
        ts = [cut(t) for t in inverse]
        mid = [dot(cut(jnp.where(mask, low_, 0.0)), t) for low_, t in zip(lowers, ts)]
        inverse = [t - dot(tc, cut(x)) for t, tc, x in zip(inverse, ts, mid)]
        size *= 2
    cut, dot = product(LEVELS["s"])
    solved = []
    for t, (kup, kdown, qup, kend, v, beta, dec) in zip(inverse, stage):
        tc = cut(t)
        solved.append((dot(tc, cut(v * beta)), dot(tc, cut(kup * beta))))
    cut, dot = product(LEVELS["m"])
    for (chunk, h), (vw, kw), at, (kup, kdown, qup, kend, v, beta, dec) in zip(places, solved, attends, stage):
        vc, kc, ac, ec = cut(vw), cut(kw), cut(at), cut(kend)
        slot = chunk * heads + h
        p_s[slot] = dot(ac, vc)
        q_s[slot] = qup - dot(ac, kc)
        m_s[slot] = eye * dec - dot(ec, kc, TN)
        b_s[slot] = dot(ec, vc, TN)


def run_states(chunks, me, heads, refs, low_s, terms, states, put):
    gu, gain = refs
    m_s, b_s, p_s, q_s = terms
    C = CHUNK
    width = heads * DK
    cut, dot = product(LEVELS["c"])
    for h in range(heads):
        states[h] = jnp.zeros((DK, DK), jnp.float32)

    def step(chunk, carry):
        for h in range(heads):
            slot = chunk * heads + h
            s = cut(states[h])
            core = p_s[slot] + dot(cut(q_s[slot]), s)
            states[h] = dot(cut(m_s[slot]), s) + b_s[slot]
            at = pl.multiple_of(me * width + h * DK, DK)
            gate = sigmoid(mm(low_s[pl.ds(pl.multiple_of(chunk * C, C), C), DK:], gu[:, pl.ds(at, DK)]))
            core = core * lax.rsqrt(jnp.mean(core * core, axis=-1, keepdims=True) + 1e-06) * gain[...]
            put(chunk, h, low(core * gate))
        return carry

    lax.fori_loop(0, chunks, step, 0)


MESH = pl.DeviceIdType.MESH


def ring_place(device, n):
    return jnp.where(device % 2 == 0, device // 2, n - 1 - device // 2)


def ring_device(place, n):
    return jnp.where(place < n // 2, 2 * place, 2 * (n - 1 - place) + 1)


def greet(n):
    me, rep = lax.axis_index("seq"), lax.axis_index("rep")
    barrier = pltpu.get_barrier_semaphore()
    for k in range(1, n):
        pl.semaphore_signal(barrier, inc=1, device_id={"seq": (me + k) % n}, device_id_type=MESH)
    for other in ((rep + 2) % 4, rep + 1 - 2 * (rep % 2)):
        pl.semaphore_signal(barrier, inc=1, device_id={"rep": other}, device_id_type=MESH)
    pl.semaphore_wait(barrier, n + 1)


def remote(src, dst, sems, k, to):
    return pltpu.make_async_remote_copy(
        src_ref=src, dst_ref=dst, send_sem=sems[0].at[k], recv_sem=sems[1].at[k], device_id=to, device_id_type=MESH
    )


def ring_copies(n, blocks, sems):
    me = lax.axis_index("seq")
    place = ring_place(me, n)
    right = {"seq": ring_device((place + 1) % n, n)}
    left = {"seq": ring_device((place + n - 1) % n, n)}
    half = blocks.shape[1] // 2
    steps = []
    for k in range(n // 2):
        goes_right = blocks.at[ring_device((place + n - k) % n, n)]
        goes_left = blocks.at[ring_device((place + k) % n, n)]
        comes_left = blocks.at[ring_device((place + n - k - 1) % n, n)]
        comes_right = blocks.at[ring_device((place + k + 1) % n, n)]
        if k == n // 2 - 1:
            goes_right, comes_left = goes_right.at[pl.ds(0, half)], comes_left.at[pl.ds(0, half)]
            goes_left, comes_right = goes_left.at[pl.ds(half, half)], comes_right.at[pl.ds(half, half)]
        steps.append(
            (
                remote(goes_right, goes_right, sems, 2 * k, right),
                remote(goes_left, goes_left, sems, 2 * k + 1, left),
                remote(comes_left, comes_left, sems, 2 * k, left),
                remote(comes_right, comes_right, sems, 2 * k + 1, right),
            )
        )
    return steps


class WeightMoves:
    def __init__(self, n, source, held, sems, local_sems):
        self.n, self.held = n, held
        me, rep = lax.axis_index("seq"), lax.axis_index("rep")
        width = held.shape[2]
        share = held.shape[1] // 4
        inverse = pow(3, -1, n)
        across, beside = (rep + 2) % 4, rep + 1 - 2 * (rep % 2)
        rows = lambda r: pl.ds(pl.multiple_of(r * share, 16), share)
        self.out, self.sent_here, self.came_here, self.local = [], [], [], []
        self.to_across, self.to_beside, self.onward = [], [], []
        self.from_across, self.from_beside, self.from_onward = [], [], []
        for j in range(3):
            piece = source.at[rows(rep), j * width : (j + 1) * width]
            mine = held.at[j, rows(rep)]
            to = (3 * me + j) % n
            self.sent_here.append(to == me)
            self.came_here.append((inverse * (me + n - j)) % n == me)
            self.out.append(remote(piece, mine, sems, j, {"seq": to}))
            self.local.append(pltpu.make_async_copy(piece, mine, local_sems.at[j]))
            self.to_across.append(remote(mine, mine, sems, 3 + j, {"rep": across}))
            self.to_beside.append(remote(mine, mine, sems, 6 + j, {"rep": beside}))
            over = held.at[j, rows(across)]
            self.from_across.append(remote(over, over, sems, 3 + j, {"rep": across}))
            self.onward.append(remote(over, over, sems, 9 + j, {"rep": beside}))
            near = held.at[j, rows(beside)]
            self.from_beside.append(remote(near, near, sems, 6 + j, {"rep": beside}))
            far = held.at[j, rows((beside + 2) % 4)]
            self.from_onward.append(remote(far, far, sems, 9 + j, {"rep": beside}))

    def begin(self):
        for j in range(3):
            pl.when(self.sent_here[j])(self.local[j].start)
            pl.when(jnp.logical_not(self.sent_here[j]))(self.out[j].start)

    def spread(self):
        for j in range(3):
            pl.when(self.came_here[j])(self.local[j].wait)
            pl.when(jnp.logical_not(self.came_here[j]))(self.out[j].wait_recv)
            self.to_across[j].start()
            self.to_beside[j].start()

    def pass_on(self):
        for j in range(3):
            self.from_across[j].wait_recv()
            self.onward[j].start()

    def finish(self):
        for j in range(3):
            self.from_beside[j].wait_recv()
            self.from_onward[j].wait_recv()

    def sent(self):
        for j in range(3):
            pl.when(jnp.logical_not(self.sent_here[j]))(self.out[j].wait_send)
            self.to_across[j].wait_send()
            self.to_beside[j].wait_send()
            self.onward[j].wait_send()


def gather_kernel(n, tok, w, blocks, held, tok_send, tok_recv, w_send, w_recv, local):
    me = lax.axis_index("seq")
    own = pltpu.make_async_copy(tok, blocks.at[me], local.at[3])
    own.start()
    greet(n)
    moves = WeightMoves(n, w, held, (w_send, w_recv), local)
    moves.begin()
    own.wait()
    steps = ring_copies(n, blocks, (tok_send, tok_recv))
    for k, (right, left, came_left, came_right) in enumerate(steps):
        right.start()
        left.start()
        if k == 0:
            moves.spread()
        if k == 2:
            moves.pass_on()
        came_left.wait_recv()
        came_right.wait_recv()
    moves.finish()
    moves.sent()
    for right, left, came_left, came_right in steps:
        right.wait_send()
        left.wait_send()


def gathered(tokens, qkv_weight, n, width):
    depth = qkv_weight.shape[0]
    anywhere = pl.BlockSpec(memory_space=pl.ANY)
    return pl.pallas_call(
        functools.partial(gather_kernel, n),
        out_shape=[
            jax.ShapeDtypeStruct((n,) + tokens.shape, tokens.dtype),
            jax.ShapeDtypeStruct((3, depth, width), qkv_weight.dtype),
        ],
        in_specs=[anywhere] * 2,
        out_specs=[anywhere] * 2,
        scratch_shapes=[
            pltpu.SemaphoreType.DMA((n,)),
            pltpu.SemaphoreType.DMA((n,)),
            pltpu.SemaphoreType.DMA((12,)),
            pltpu.SemaphoreType.DMA((12,)),
            pltpu.SemaphoreType.DMA((4,)),
        ],
        compiler_params=pltpu.CompilerParams(collective_id=0, has_side_effects=True),
    )(tokens, qkv_weight)


def heads_kernel(n, heads, tok, w, conv, dd, du, rate, bw, bs, gd, gu, gain, out, mixed_s, low_s, beta_s, m_s, b_s, p_s, q_s, states):
    me = lax.axis_index("seq")
    count = tok.shape[0]
    chunks = count // CHUNK
    mixed_s[0:8, :] = jnp.zeros((8, mixed_s.shape[1]), jnp.float32)

    def w_at(t):
        return w[lax.rem(t * n + me, 3)]

    def first(c, carry):
        rows = pl.multiple_of(c * CHUNK, CHUNK)
        project(rows, tok[pl.ds(rows, CHUNK), :], w_at, (dd, gd, bw, bs), mixed_s, low_s, beta_s)
        return carry

    lax.fori_loop(0, chunks, first, 0)

    def second(c, carry):
        places = [(c * 2 + i, h) for i in range(2) for h in range(heads)]
        chunk_terms(places, me, heads, (conv, du, rate), (mixed_s, low_s, beta_s), (m_s, b_s, p_s, q_s))
        return carry

    lax.fori_loop(0, chunks // 2, second, 0)

    def put(chunk, h, value):
        out[pl.ds(pl.multiple_of(chunk * CHUNK, CHUNK), CHUNK), h * DK : (h + 1) * DK] = value

    run_states(chunks, me, heads, (gu, gain), low_s, (m_s, b_s, p_s, q_s), states, put)


def heads_split(tokens, qkv_weight, conv_weight, decay_down, decay_up, decay_rate, beta_weight, beta_scale, gate_down, gate_up, norm_gain):
    n = lax.axis_size("seq")
    heads = H // n
    width = heads * DK
    blocks, weight = gathered(tokens, qkv_weight, n, width)
    everything = blocks.reshape(-1, tokens.shape[1])
    count = everything.shape[0]
    slots = count // CHUNK * heads
    square = pltpu.VMEM((slots, DK, DK), jnp.float32)
    attended = pl.pallas_call(
        functools.partial(heads_kernel, n, heads),
        out_shape=jax.ShapeDtypeStruct((count, width), jnp.bfloat16),
        in_specs=[pl.BlockSpec(memory_space=pltpu.VMEM)] * 11,
        out_specs=pl.BlockSpec(memory_space=pltpu.VMEM),
        scratch_shapes=[
            pltpu.VMEM((count + 8, 3 * width), jnp.float32),
            pltpu.VMEM((count, 2 * DK), jnp.bfloat16),
            pltpu.VMEM((count, H), jnp.float32),
            square, square, square, square,
            pltpu.VMEM((heads, DK, DK), jnp.float32),
        ],
        compiler_params=pltpu.CompilerParams(vmem_limit_bytes=48 * 2**20),
    )(everything, weight, conv_weight, decay_down, decay_up, decay_rate.reshape(1, -1), beta_weight, beta_scale.reshape(1, -1), gate_down, gate_up, norm_gain.reshape(1, -1))
    return lax.all_to_all(attended, "seq", 0, 1, tiled=True)


def by_heads(mesh):
    n, reps = mesh.shape["seq"], mesh.shape["rep"]
    return H % n == 0 and n % 3 != 0 and n % 2 == 0 and reps == 4


def solution(mesh):
    in_specs = (
        P(("rep", "seq"), None),
        P(None, "seq"),
        P(),
        P(),
        P(),
        P(),
        P(),
        P(),
        P(),
        P(),
        P(),
    )
    out_specs = P(("rep", "seq"), None)
    return jax.shard_map(
        heads_split if by_heads(mesh) else tokens_split, mesh=mesh, in_specs=in_specs, out_specs=out_specs, check_vma=False
    )
```

```python
import functools
import jax
import jax.numpy as jnp
from jax import lax
from jax.experimental import pallas as pl
from jax.experimental.pallas import tpu as pltpu
from jax.sharding import PartitionSpec as P

H = 16
DK = 128
CONV = 4
BLOCK = 64


precise = lax.Precision.HIGHEST


def from_behind(block, axis, distance):
    devices = range(lax.axis_size(axis))
    route = [(i - distance, i) for i in devices if i - distance in devices]
    return lax.ppermute(block, axis, route)


def carried_in(x, axis, combine, identity):
    devices, mine = (lax.axis_size(axis), lax.axis_index(axis))
    everything = jax.tree.map(lambda part: lax.all_gather(part, axis), x)
    start = jax.tree.map(
        lambda part, zero: jnp.broadcast_to(jnp.asarray(zero, part.dtype), part.shape), x, identity
    )

    def lap(k, before):
        reached = k < mine
        new = combine(before, jax.tree.map(lambda part: part[k], everything))
        return jax.tree.map(lambda a, b: jnp.where(reached, a, b), new, before)

    return lax.fori_loop(0, devices, lap, start)


def unit_rows(vector):
    return vector * lax.rsqrt(jnp.sum(vector * vector, axis=-1, keepdims=True) + 1e-06)


def features(padded, count, conv_weight):
    combined = conv_weight[0] * padded[0:count].astype(jnp.float32)
    for offset in range(1, CONV):
        combined = combined + conv_weight[offset] * padded[offset : offset + count].astype(
            jnp.float32
        )
    active = jax.nn.silu(combined).reshape(count, 3, H, DK)
    query = unit_rows(active[:, 0]) * DK ** (-0.5)
    keys = unit_rows(active[:, 1])
    values = active[:, 2]
    return (query, keys, values)


def gates(tokens, decay_down, decay_up, decay_rate, beta_weight, beta_scale, gate_down, gate_up):
    beta = beta_scale * jax.nn.sigmoid(
        jnp.dot(tokens, beta_weight, preferred_element_type=jnp.float32)
    )
    decay_low = jnp.dot(tokens, decay_down, preferred_element_type=jnp.float32).astype(jnp.bfloat16)
    logdec = -decay_rate * jax.nn.sigmoid(
        jnp.dot(decay_low, decay_up, preferred_element_type=jnp.float32)
    )
    gate_low = jnp.dot(tokens, gate_down, preferred_element_type=jnp.float32).astype(jnp.bfloat16)
    gate_value = jax.nn.sigmoid(jnp.dot(gate_low, gate_up, preferred_element_type=jnp.float32))
    return (beta, logdec, gate_value)


def to_blocks(array, count):
    return array.reshape(count // BLOCK, BLOCK, H, array.shape[-1]).transpose(0, 2, 1, 3)


def block_terms(query, keys, values, beta, logdec):
    log_sum = jnp.cumsum(logdec, axis=2)
    grow = jnp.exp(log_sum)
    keys_up = keys * grow
    keys_down = keys * jnp.exp(-log_sum)
    query_up = query * grow
    keys_end = keys * jnp.exp(log_sum[:, :, -1:, :] - log_sum)
    length = query.shape[2]
    rows = lax.broadcasted_iota(jnp.int32, (length, length), 0)
    columns = lax.broadcasted_iota(jnp.int32, (length, length), 1)
    scores = jnp.einsum("nhic,nhjc->nhij", keys_up, keys_down, precision=precise) * beta[..., None]
    system = jnp.where(rows > columns, scores, 0.0) + jnp.eye(length, dtype=jnp.float32)
    right_side = jnp.concatenate([values, keys_up], axis=-1) * beta[..., None]
    solved = jax.scipy.linalg.solve_triangular(system, right_side, lower=True, unit_diagonal=True)
    values_w = solved[..., :DK]
    keys_w = solved[..., DK:]
    attend = jnp.where(
        rows >= columns, jnp.einsum("nhic,nhjc->nhij", query_up, keys_down, precision=precise), 0.0
    )
    decay_end = jnp.exp(log_sum[:, :, -1, :])
    return (query_up, keys_end, values_w, keys_w, attend, decay_end)


def advance(state, inputs):
    query_up, keys_end, values_w, keys_w, attend, decay_end = inputs
    update = values_w - jnp.einsum("hcd,hde->hce", keys_w, state, precision=precise)
    output = jnp.einsum("hcd,hde->hce", query_up, state, precision=precise)
    output = output + jnp.einsum("hij,hje->hie", attend, update, precision=precise)
    state = decay_end[..., None] * state + jnp.einsum(
        "hcd,hce->hde", keys_end, update, precision=precise
    )
    return (state, output)


def matmul(left, right):
    return jnp.einsum("...de,...ef->...df", left, right, precision=precise)


def fold_block(carry, inputs):
    matrix, offset = carry
    keys_end, keys_w, values_w, decay_end = inputs
    eye_block = jnp.eye(DK, dtype=jnp.float32)
    block_matrix = decay_end[..., None] * eye_block - jnp.einsum(
        "hcd,hce->hde", keys_end, keys_w, precision=precise
    )
    block_offset = jnp.einsum("hcd,hce->hde", keys_end, values_w, precision=precise)
    return ((matmul(block_matrix, matrix), matmul(block_matrix, offset) + block_offset), None)


def join_pairs(first, second):
    return (matmul(second[0], first[0]), matmul(second[0], first[1]) + second[1])


def finish(core, gate_value, norm_gain, count):
    scaled = core * lax.rsqrt(jnp.mean(core * core, axis=-1, keepdims=True) + 1e-06) * norm_gain
    return (scaled.reshape(count, H * DK) * gate_value).astype(jnp.bfloat16)


def tokens_split(
    tokens,
    qkv_weight,
    conv_weight,
    decay_down,
    decay_up,
    decay_rate,
    beta_weight,
    beta_scale,
    gate_down,
    gate_up,
    norm_gain,
):
    count = tokens.shape[0]
    mixed = jnp.dot(
        tokens,
        lax.all_gather(qkv_weight, "seq", axis=1, tiled=True),
        preferred_element_type=jnp.float32,
    ).astype(jnp.bfloat16)
    earlier = from_behind(mixed[count - (CONV - 1) :], "seq", 1)
    padded = jnp.concatenate([earlier, mixed], axis=0)
    query, keys, values = features(padded, count, conv_weight)
    beta, logdec, gate_value = gates(
        tokens, decay_down, decay_up, decay_rate, beta_weight, beta_scale, gate_down, gate_up
    )
    beta_blocks = beta.reshape(count // BLOCK, BLOCK, H).transpose(0, 2, 1)
    terms = block_terms(
        to_blocks(query, count),
        to_blocks(keys, count),
        to_blocks(values, count),
        beta_blocks,
        to_blocks(logdec.reshape(count, H, DK), count),
    )
    query_up, keys_end, values_w, keys_w, attend, decay_end = terms
    identity = jnp.broadcast_to(jnp.eye(DK, dtype=jnp.float32), (H, DK, DK))
    zeroed = jnp.zeros((H, DK, DK), jnp.float32)
    (matrix, offset), unused = lax.scan(
        fold_block, (identity, zeroed), (keys_end, keys_w, values_w, decay_end)
    )

    def combine(earlier_pair, later_pair):
        return join_pairs(earlier_pair, later_pair)

    prefix = carried_in((matrix, offset), "seq", combine, (identity, zeroed))
    incoming = prefix[1]
    final_state, outputs = lax.scan(advance, incoming, terms)
    core = outputs.transpose(0, 2, 1, 3).reshape(count, H, DK)
    return finish(core, gate_value, norm_gain, count)


CHUNK = 128
NN = (((1,), (0,)), ((), ()))
NT = (((1,), (1,)), ((), ()))
TN = (((0,), (0,)), ((), ()))


def mm(a, b, dims=NN):
    return lax.dot_general(a, b, dims, preferred_element_type=jnp.float32)


def low(a):
    return a.astype(jnp.bfloat16)


def split(a):
    top = low(a)
    return top, low(a - top.astype(jnp.float32))


def mm3(a, b, dims=NN):
    (ah, al), (bh, bl) = a, b
    return mm(ah, bh, dims) + (mm(ah, bl, dims) + mm(al, bh, dims))


def product(level):
    if level == 1:
        return low, mm
    return split, mm3


LEVELS = {"g": 3, "t": 1, "s": 3, "m": 3, "c": 3}


def sigmoid(u):
    return 1.0 / (1.0 + jnp.exp(-u))


def project(rows, tok, w_at, gate_refs, mixed_s, low_s, beta_s):
    dd, gd, bw, bs = gate_refs
    width = w_at(0).shape[1]
    for t in range(3):
        got = mm(tok, w_at(t)).astype(jnp.bfloat16).astype(jnp.float32)
        mixed_s[pl.ds(pl.multiple_of(rows + 8, 8), tok.shape[0]), t * width : (t + 1) * width] = got
    low_s[pl.ds(rows, tok.shape[0]), :DK] = low(mm(tok, dd[...]))
    low_s[pl.ds(rows, tok.shape[0]), DK:] = low(mm(tok, gd[...]))
    beta_s[pl.ds(rows, tok.shape[0]), :] = bs[...] * sigmoid(mm(tok, bw[...]))


def chunk_terms(places, me, heads, refs, scratch, terms):
    conv, du, rate = refs
    mixed_s, low_s, beta_s = scratch
    m_s, b_s, p_s, q_s = terms
    C = CHUNK
    width = heads * DK
    rows = lax.broadcasted_iota(jnp.int32, (C, C), 0)
    cols = lax.broadcasted_iota(jnp.int32, (C, C), 1)
    tril = jnp.where(rows >= cols, 1.0, 0.0).astype(jnp.bfloat16)
    eye = jnp.where(rows == cols, 1.0, 0.0)
    total = conv.shape[1] // 3

    def part(t, chunk, h):
        at = pl.multiple_of(t * total + me * width + h * DK, DK)
        acc = None
        near = mixed_s[pl.ds(pl.multiple_of(chunk * C, C), C + 8), t * width + h * DK : t * width + (h + 1) * DK]
        for j in range(CONV):
            got = near[8 - (CONV - 1) + j : 8 - (CONV - 1) + j + C]
            term = conv[j : j + 1, pl.ds(at, DK)] * got
            acc = term if acc is None else acc + term
        return acc * sigmoid(acc)

    def unit(a):
        return a * lax.rsqrt(jnp.sum(a * a, axis=-1, keepdims=True) + 1e-06)

    stage = []
    for chunk, h in places:
        q = unit(part(0, chunk, h)) * DK ** (-0.5)
        k = unit(part(1, chunk, h))
        v = part(2, chunk, h)
        at = pl.multiple_of(me * width + h * DK, DK)
        down = low_s[pl.ds(pl.multiple_of(chunk * C, C), C), :DK]
        logdec = -rate[:, pl.ds(at, DK)] * sigmoid(mm(down, du[:, pl.ds(at, DK)]))
        every = beta_s[pl.ds(pl.multiple_of(chunk * C, C), C), :]
        lane = lax.broadcasted_iota(jnp.int32, every.shape, 1)
        beta = jnp.sum(jnp.where(lane == me * heads + h, every, 0.0), axis=1, keepdims=True)
        lh, ll = split(logdec)
        ls = mm(tril, lh) + mm(tril, ll)
        last = ls[C - 1 : C, :]
        grow = jnp.exp(ls)
        kup = k * grow
        stage.append((kup, k * jnp.exp(-ls), q * grow, k * jnp.exp(last - ls), v, beta, jnp.exp(last)))
    cut, dot = product(LEVELS["g"])
    lowers, attends = [], []
    for kup, kdown, qup, kend, v, beta, dec in stage:
        kd = cut(kdown)
        lowers.append(jnp.where(rows > cols, dot(cut(kup), kd, NT) * beta, 0.0))
        attends.append(jnp.where(rows >= cols, dot(cut(qup), kd, NT), 0.0))
    cut, dot = product(LEVELS["t"])
    inverse = [eye - jnp.where(rows // 2 == cols // 2, low_, 0.0) for low_ in lowers]
    size = 2
    while size < C:
        mask = jnp.logical_and(rows // (2 * size) == cols // (2 * size), rows // size != cols // size)
        ts = [cut(t) for t in inverse]
        mid = [dot(cut(jnp.where(mask, low_, 0.0)), t) for low_, t in zip(lowers, ts)]
        inverse = [t - dot(tc, cut(x)) for t, tc, x in zip(inverse, ts, mid)]
        size *= 2
    cut, dot = product(LEVELS["s"])
    solved = []
    for t, (kup, kdown, qup, kend, v, beta, dec) in zip(inverse, stage):
        tc = cut(t)
        solved.append((dot(tc, cut(v * beta)), dot(tc, cut(kup * beta))))
    cut, dot = product(LEVELS["m"])
    for (chunk, h), (vw, kw), at, (kup, kdown, qup, kend, v, beta, dec) in zip(places, solved, attends, stage):
        vc, kc, ac, ec = cut(vw), cut(kw), cut(at), cut(kend)
        slot = chunk * heads + h
        p_s[slot] = dot(ac, vc)
        q_s[slot] = qup - dot(ac, kc)
        m_s[slot] = eye * dec - dot(ec, kc, TN)
        b_s[slot] = dot(ec, vc, TN)


def run_states(chunks, me, heads, refs, low_s, terms, states, put, post):
    gu, gain = refs
    m_s, b_s, p_s, q_s = terms
    C = CHUNK
    width = heads * DK
    cut, dot = product(LEVELS["c"])
    for h in range(heads):
        states[h] = jnp.zeros((DK, DK), jnp.float32)

    def step(chunk, carry):
        for h in range(heads):
            slot = chunk * heads + h
            s = cut(states[h])
            core = p_s[slot] + dot(cut(q_s[slot]), s)
            states[h] = dot(cut(m_s[slot]), s) + b_s[slot]
            at = pl.multiple_of(me * width + h * DK, DK)
            gate = sigmoid(mm(low_s[pl.ds(pl.multiple_of(chunk * C, C), C), DK:], gu[:, pl.ds(at, DK)]))
            core = core * lax.rsqrt(jnp.mean(core * core, axis=-1, keepdims=True) + 1e-06) * gain[...]
            put(chunk, h, low(core * gate))
        post(chunk)
        return carry

    lax.fori_loop(0, chunks, step, 0)


MESH = pl.DeviceIdType.MESH


def ring_place(device, n):
    return jnp.where(device % 2 == 0, device // 2, n - 1 - device // 2)


def ring_device(place, n):
    return jnp.where(place < n // 2, 2 * place, 2 * (n - 1 - place) + 1)


def greet(n):
    me, rep = lax.axis_index("seq"), lax.axis_index("rep")
    barrier = pltpu.get_barrier_semaphore()
    for k in range(1, n):
        pl.semaphore_signal(barrier, inc=1, device_id={"seq": (me + k) % n}, device_id_type=MESH)
    for other in ((rep + 2) % 4, rep + 1 - 2 * (rep % 2)):
        pl.semaphore_signal(barrier, inc=1, device_id={"rep": other}, device_id_type=MESH)
    pl.semaphore_wait(barrier, n + 1)


def remote(src, dst, sems, k, to):
    return pltpu.make_async_remote_copy(
        src_ref=src, dst_ref=dst, send_sem=sems[0].at[k], recv_sem=sems[1].at[k], device_id=to, device_id_type=MESH
    )


def ring_copies(n, blocks, sems):
    me = lax.axis_index("seq")
    place = ring_place(me, n)
    right = {"seq": ring_device((place + 1) % n, n)}
    left = {"seq": ring_device((place + n - 1) % n, n)}
    half = blocks.shape[1] // 2
    steps = []
    for k in range(n // 2):
        goes_right = blocks.at[ring_device((place + n - k) % n, n)]
        goes_left = blocks.at[ring_device((place + k) % n, n)]
        comes_left = blocks.at[ring_device((place + n - k - 1) % n, n)]
        comes_right = blocks.at[ring_device((place + k + 1) % n, n)]
        if k == n // 2 - 1:
            goes_right, comes_left = goes_right.at[pl.ds(0, half)], comes_left.at[pl.ds(0, half)]
            goes_left, comes_right = goes_left.at[pl.ds(half, half)], comes_right.at[pl.ds(half, half)]
        steps.append(
            (
                remote(goes_right, goes_right, sems, 2 * k, right),
                remote(goes_left, goes_left, sems, 2 * k + 1, left),
                remote(comes_left, comes_left, sems, 2 * k, left),
                remote(comes_right, comes_right, sems, 2 * k + 1, right),
            )
        )
    return steps


class WeightMoves:
    def __init__(self, n, source, held, sems, local_sems):
        self.n, self.held = n, held
        me, rep = lax.axis_index("seq"), lax.axis_index("rep")
        width = held.shape[2]
        share = held.shape[1] // 4
        inverse = pow(3, -1, n)
        across, beside = (rep + 2) % 4, rep + 1 - 2 * (rep % 2)
        rows = lambda r: pl.ds(pl.multiple_of(r * share, 16), share)
        self.out, self.sent_here, self.came_here, self.local = [], [], [], []
        self.to_across, self.to_beside, self.onward = [], [], []
        self.from_across, self.from_beside, self.from_onward = [], [], []
        for j in range(3):
            piece = source.at[rows(rep), j * width : (j + 1) * width]
            mine = held.at[j, rows(rep)]
            to = (3 * me + j) % n
            self.sent_here.append(to == me)
            self.came_here.append((inverse * (me + n - j)) % n == me)
            self.out.append(remote(piece, mine, sems, j, {"seq": to}))
            self.local.append(pltpu.make_async_copy(piece, mine, local_sems.at[j]))
            self.to_across.append(remote(mine, mine, sems, 3 + j, {"rep": across}))
            self.to_beside.append(remote(mine, mine, sems, 6 + j, {"rep": beside}))
            over = held.at[j, rows(across)]
            self.from_across.append(remote(over, over, sems, 3 + j, {"rep": across}))
            self.onward.append(remote(over, over, sems, 9 + j, {"rep": beside}))
            near = held.at[j, rows(beside)]
            self.from_beside.append(remote(near, near, sems, 6 + j, {"rep": beside}))
            far = held.at[j, rows((beside + 2) % 4)]
            self.from_onward.append(remote(far, far, sems, 9 + j, {"rep": beside}))

    def begin(self):
        for j in range(3):
            pl.when(self.sent_here[j])(self.local[j].start)
            pl.when(jnp.logical_not(self.sent_here[j]))(self.out[j].start)

    def spread(self):
        for j in range(3):
            pl.when(self.came_here[j])(self.local[j].wait)
            pl.when(jnp.logical_not(self.came_here[j]))(self.out[j].wait_recv)
            self.to_across[j].start()
            self.to_beside[j].start()

    def pass_on(self):
        for j in range(3):
            self.from_across[j].wait_recv()
            self.onward[j].start()

    def finish(self):
        for j in range(3):
            self.from_beside[j].wait_recv()
            self.from_onward[j].wait_recv()

    def sent(self):
        for j in range(3):
            pl.when(jnp.logical_not(self.sent_here[j]))(self.out[j].wait_send)
            self.to_across[j].wait_send()
            self.to_beside[j].wait_send()
            self.onward[j].wait_send()


def gather_kernel(n, tok, w, blocks, held, tok_send, tok_recv, w_send, w_recv, local):
    me = lax.axis_index("seq")
    own = pltpu.make_async_copy(tok, blocks.at[me], local.at[3])
    own.start()
    greet(n)
    moves = WeightMoves(n, w, held, (w_send, w_recv), local)
    moves.begin()
    own.wait()
    steps = ring_copies(n, blocks, (tok_send, tok_recv))
    for k, (right, left, came_left, came_right) in enumerate(steps):
        right.start()
        left.start()
        if k == 0:
            moves.spread()
        if k == 2:
            moves.pass_on()
        came_left.wait_recv()
        came_right.wait_recv()
    moves.finish()
    moves.sent()
    for right, left, came_left, came_right in steps:
        right.wait_send()
        left.wait_send()


def gathered(tokens, qkv_weight, n, width):
    depth = qkv_weight.shape[0]
    anywhere = pl.BlockSpec(memory_space=pl.ANY)
    return pl.pallas_call(
        functools.partial(gather_kernel, n),
        out_shape=[
            jax.ShapeDtypeStruct((n,) + tokens.shape, tokens.dtype),
            jax.ShapeDtypeStruct((3, depth, width), qkv_weight.dtype),
        ],
        in_specs=[anywhere] * 2,
        out_specs=[anywhere] * 2,
        scratch_shapes=[
            pltpu.SemaphoreType.DMA((n,)),
            pltpu.SemaphoreType.DMA((n,)),
            pltpu.SemaphoreType.DMA((12,)),
            pltpu.SemaphoreType.DMA((12,)),
            pltpu.SemaphoreType.DMA((4,)),
        ],
        compiler_params=pltpu.CompilerParams(collective_id=0, has_side_effects=True),
    )(tokens, qkv_weight)


def heads_kernel(n, heads, tok, w, conv, dd, du, rate, bw, bs, gd, gu, gain, out, mixed_s, low_s, beta_s, m_s, b_s, p_s, q_s, states, stage, send, recv, local):
    me = lax.axis_index("seq")
    count = tok.shape[0]
    chunks = count // CHUNK
    width = heads * DK
    greet(n)
    mixed_s[0:8, :] = jnp.zeros((8, mixed_s.shape[1]), jnp.float32)

    def w_at(t):
        return w[lax.rem(t * n + me, 3)]

    def first(c, carry):
        rows = pl.multiple_of(c * CHUNK, CHUNK)
        project(rows, tok[pl.ds(rows, CHUNK), :], w_at, (dd, gd, bw, bs), mixed_s, low_s, beta_s)
        return carry

    lax.fori_loop(0, chunks, first, 0)

    def second(c, carry):
        places = [(c * 2 + i, h) for i in range(2) for h in range(heads)]
        chunk_terms(places, me, heads, (conv, du, rate), (mixed_s, low_s, beta_s), (m_s, b_s, p_s, q_s))
        return carry

    lax.fori_loop(0, chunks // 2, second, 0)

    def columns(device):
        return out.at[:, pl.ds(pl.multiple_of(device * width, width), width)]

    def parcel(to):
        return pltpu.make_async_remote_copy(
            src_ref=stage.at[to], dst_ref=columns(me), send_sem=send.at[to], recv_sem=recv.at[me],
            device_id={"seq": to}, device_id_type=MESH,
        )

    def put(chunk, h, value):
        stage[chunk, :, h * DK : (h + 1) * DK] = value

    def post(chunk):
        pl.when(chunk != me)(lambda: parcel(chunk).start())

    run_states(chunks, me, heads, (gu, gain), low_s, (m_s, b_s, p_s, q_s), states, put, post)
    own = pltpu.make_async_copy(stage.at[me], columns(me), local.at[0])
    own.start()
    own.wait()
    for k in range(1, n):
        other = (me + k) % n
        parcel(other).wait_send()
        pltpu.make_async_remote_copy(
            src_ref=stage.at[other], dst_ref=columns(other), send_sem=send.at[other], recv_sem=recv.at[other],
            device_id={"seq": other}, device_id_type=MESH,
        ).wait_recv()


def heads_split(tokens, qkv_weight, conv_weight, decay_down, decay_up, decay_rate, beta_weight, beta_scale, gate_down, gate_up, norm_gain):
    n = lax.axis_size("seq")
    heads = H // n
    width = heads * DK
    blocks, weight = gathered(tokens, qkv_weight, n, width)
    everything = blocks.reshape(-1, tokens.shape[1])
    count = everything.shape[0]
    slots = count // CHUNK * heads
    square = pltpu.VMEM((slots, DK, DK), jnp.float32)
    attended = pl.pallas_call(
        functools.partial(heads_kernel, n, heads),
        out_shape=jax.ShapeDtypeStruct((tokens.shape[0], H * DK), jnp.bfloat16),
        in_specs=[pl.BlockSpec(memory_space=pltpu.VMEM)] * 11,
        out_specs=pl.BlockSpec(memory_space=pltpu.VMEM),
        scratch_shapes=[
            pltpu.VMEM((count + 8, 3 * width), jnp.float32),
            pltpu.VMEM((count, 2 * DK), jnp.bfloat16),
            pltpu.VMEM((count, H), jnp.float32),
            square, square, square, square,
            pltpu.VMEM((heads, DK, DK), jnp.float32),
            pltpu.VMEM((n, CHUNK, width), jnp.bfloat16),
            pltpu.SemaphoreType.DMA((n,)),
            pltpu.SemaphoreType.DMA((n,)),
            pltpu.SemaphoreType.DMA((1,)),
        ],
        compiler_params=pltpu.CompilerParams(collective_id=1, has_side_effects=True, vmem_limit_bytes=48 * 2**20),
    )(everything, weight, conv_weight, decay_down, decay_up, decay_rate.reshape(1, -1), beta_weight, beta_scale.reshape(1, -1), gate_down, gate_up, norm_gain.reshape(1, -1))
    return attended


def layer(tokens, *rest):
    n, reps = lax.axis_size("seq"), lax.axis_size("rep")
    fits = H % n == 0 and n % 3 != 0 and n % 2 == 0 and reps == 4 and tokens.shape[0] == CHUNK
    return (heads_split if fits else tokens_split)(tokens, *rest)


def solution(mesh):
    in_specs = (
        P(("rep", "seq"), None),
        P(None, "seq"),
        P(),
        P(),
        P(),
        P(),
        P(),
        P(),
        P(),
        P(),
        P(),
    )
    out_specs = P(("rep", "seq"), None)
    return jax.shard_map(
        layer, mesh=mesh, in_specs=in_specs, out_specs=out_specs, check_vma=False
    )
```

```python
import functools
import jax
import jax.numpy as jnp
from jax import lax
from jax.experimental import pallas as pl
from jax.experimental.pallas import tpu as pltpu
from jax.sharding import PartitionSpec as P

H = 16
DK = 128
CONV = 4
BLOCK = 64


precise = lax.Precision.HIGHEST


def from_behind(block, axis, distance):
    devices = range(lax.axis_size(axis))
    route = [(i - distance, i) for i in devices if i - distance in devices]
    return lax.ppermute(block, axis, route)


def carried_in(x, axis, combine, identity):
    devices, mine = (lax.axis_size(axis), lax.axis_index(axis))
    everything = jax.tree.map(lambda part: lax.all_gather(part, axis), x)
    start = jax.tree.map(
        lambda part, zero: jnp.broadcast_to(jnp.asarray(zero, part.dtype), part.shape), x, identity
    )

    def lap(k, before):
        reached = k < mine
        new = combine(before, jax.tree.map(lambda part: part[k], everything))
        return jax.tree.map(lambda a, b: jnp.where(reached, a, b), new, before)

    return lax.fori_loop(0, devices, lap, start)


def unit_rows(vector):
    return vector * lax.rsqrt(jnp.sum(vector * vector, axis=-1, keepdims=True) + 1e-06)


def features(padded, count, conv_weight):
    combined = conv_weight[0] * padded[0:count].astype(jnp.float32)
    for offset in range(1, CONV):
        combined = combined + conv_weight[offset] * padded[offset : offset + count].astype(
            jnp.float32
        )
    active = jax.nn.silu(combined).reshape(count, 3, H, DK)
    query = unit_rows(active[:, 0]) * DK ** (-0.5)
    keys = unit_rows(active[:, 1])
    values = active[:, 2]
    return (query, keys, values)


def gates(tokens, decay_down, decay_up, decay_rate, beta_weight, beta_scale, gate_down, gate_up):
    beta = beta_scale * jax.nn.sigmoid(
        jnp.dot(tokens, beta_weight, preferred_element_type=jnp.float32)
    )
    decay_low = jnp.dot(tokens, decay_down, preferred_element_type=jnp.float32).astype(jnp.bfloat16)
    logdec = -decay_rate * jax.nn.sigmoid(
        jnp.dot(decay_low, decay_up, preferred_element_type=jnp.float32)
    )
    gate_low = jnp.dot(tokens, gate_down, preferred_element_type=jnp.float32).astype(jnp.bfloat16)
    gate_value = jax.nn.sigmoid(jnp.dot(gate_low, gate_up, preferred_element_type=jnp.float32))
    return (beta, logdec, gate_value)


def to_blocks(array, count):
    return array.reshape(count // BLOCK, BLOCK, H, array.shape[-1]).transpose(0, 2, 1, 3)


def block_terms(query, keys, values, beta, logdec):
    log_sum = jnp.cumsum(logdec, axis=2)
    grow = jnp.exp(log_sum)
    keys_up = keys * grow
    keys_down = keys * jnp.exp(-log_sum)
    query_up = query * grow
    keys_end = keys * jnp.exp(log_sum[:, :, -1:, :] - log_sum)
    length = query.shape[2]
    rows = lax.broadcasted_iota(jnp.int32, (length, length), 0)
    columns = lax.broadcasted_iota(jnp.int32, (length, length), 1)
    scores = jnp.einsum("nhic,nhjc->nhij", keys_up, keys_down, precision=precise) * beta[..., None]
    system = jnp.where(rows > columns, scores, 0.0) + jnp.eye(length, dtype=jnp.float32)
    right_side = jnp.concatenate([values, keys_up], axis=-1) * beta[..., None]
    solved = jax.scipy.linalg.solve_triangular(system, right_side, lower=True, unit_diagonal=True)
    values_w = solved[..., :DK]
    keys_w = solved[..., DK:]
    attend = jnp.where(
        rows >= columns, jnp.einsum("nhic,nhjc->nhij", query_up, keys_down, precision=precise), 0.0
    )
    decay_end = jnp.exp(log_sum[:, :, -1, :])
    return (query_up, keys_end, values_w, keys_w, attend, decay_end)


def advance(state, inputs):
    query_up, keys_end, values_w, keys_w, attend, decay_end = inputs
    update = values_w - jnp.einsum("hcd,hde->hce", keys_w, state, precision=precise)
    output = jnp.einsum("hcd,hde->hce", query_up, state, precision=precise)
    output = output + jnp.einsum("hij,hje->hie", attend, update, precision=precise)
    state = decay_end[..., None] * state + jnp.einsum(
        "hcd,hce->hde", keys_end, update, precision=precise
    )
    return (state, output)


def matmul(left, right):
    return jnp.einsum("...de,...ef->...df", left, right, precision=precise)


def fold_block(carry, inputs):
    matrix, offset = carry
    keys_end, keys_w, values_w, decay_end = inputs
    eye_block = jnp.eye(DK, dtype=jnp.float32)
    block_matrix = decay_end[..., None] * eye_block - jnp.einsum(
        "hcd,hce->hde", keys_end, keys_w, precision=precise
    )
    block_offset = jnp.einsum("hcd,hce->hde", keys_end, values_w, precision=precise)
    return ((matmul(block_matrix, matrix), matmul(block_matrix, offset) + block_offset), None)


def join_pairs(first, second):
    return (matmul(second[0], first[0]), matmul(second[0], first[1]) + second[1])


def finish(core, gate_value, norm_gain, count):
    scaled = core * lax.rsqrt(jnp.mean(core * core, axis=-1, keepdims=True) + 1e-06) * norm_gain
    return (scaled.reshape(count, H * DK) * gate_value).astype(jnp.bfloat16)


def tokens_split(
    tokens,
    qkv_weight,
    conv_weight,
    decay_down,
    decay_up,
    decay_rate,
    beta_weight,
    beta_scale,
    gate_down,
    gate_up,
    norm_gain,
):
    count = tokens.shape[0]
    mixed = jnp.dot(
        tokens,
        lax.all_gather(qkv_weight, "seq", axis=1, tiled=True),
        preferred_element_type=jnp.float32,
    ).astype(jnp.bfloat16)
    earlier = from_behind(mixed[count - (CONV - 1) :], "seq", 1)
    padded = jnp.concatenate([earlier, mixed], axis=0)
    query, keys, values = features(padded, count, conv_weight)
    beta, logdec, gate_value = gates(
        tokens, decay_down, decay_up, decay_rate, beta_weight, beta_scale, gate_down, gate_up
    )
    beta_blocks = beta.reshape(count // BLOCK, BLOCK, H).transpose(0, 2, 1)
    terms = block_terms(
        to_blocks(query, count),
        to_blocks(keys, count),
        to_blocks(values, count),
        beta_blocks,
        to_blocks(logdec.reshape(count, H, DK), count),
    )
    query_up, keys_end, values_w, keys_w, attend, decay_end = terms
    identity = jnp.broadcast_to(jnp.eye(DK, dtype=jnp.float32), (H, DK, DK))
    zeroed = jnp.zeros((H, DK, DK), jnp.float32)
    (matrix, offset), unused = lax.scan(
        fold_block, (identity, zeroed), (keys_end, keys_w, values_w, decay_end)
    )

    def combine(earlier_pair, later_pair):
        return join_pairs(earlier_pair, later_pair)

    prefix = carried_in((matrix, offset), "seq", combine, (identity, zeroed))
    incoming = prefix[1]
    final_state, outputs = lax.scan(advance, incoming, terms)
    core = outputs.transpose(0, 2, 1, 3).reshape(count, H, DK)
    return finish(core, gate_value, norm_gain, count)


CHUNK = 128
NN = (((1,), (0,)), ((), ()))
NT = (((1,), (1,)), ((), ()))
TN = (((0,), (0,)), ((), ()))


def mm(a, b, dims=NN):
    return lax.dot_general(a, b, dims, preferred_element_type=jnp.float32)


def low(a):
    return a.astype(jnp.bfloat16)


def split(a):
    top = low(a)
    return top, low(a - top.astype(jnp.float32))


def mm3(a, b, dims=NN):
    (ah, al), (bh, bl) = a, b
    return mm(ah, bh, dims) + (mm(ah, bl, dims) + mm(al, bh, dims))


def product(level):
    if level == 1:
        return low, mm
    return split, mm3


LEVELS = {"g": 3, "t": 1, "s": 3, "m": 3, "c": 3}


def sigmoid(u):
    return 1.0 / (1.0 + jnp.exp(-u))


def project(rows, tok, w_at, gate_refs, mixed_s, low_s, beta_s):
    dd, gd, bw, bs = gate_refs
    width = w_at(0).shape[1]
    for t in range(3):
        got = mm(tok, w_at(t)).astype(jnp.bfloat16).astype(jnp.float32)
        mixed_s[pl.ds(pl.multiple_of(rows + 8, 8), tok.shape[0]), t * width : (t + 1) * width] = got
    low_s[pl.ds(rows, tok.shape[0]), :DK] = low(mm(tok, dd[...]))
    low_s[pl.ds(rows, tok.shape[0]), DK:] = low(mm(tok, gd[...]))
    beta_s[pl.ds(rows, tok.shape[0]), :] = bs[...] * sigmoid(mm(tok, bw[...]))


def chunk_terms(places, me, heads, refs, scratch, terms):
    conv, du, rate = refs
    mixed_s, low_s, beta_s = scratch
    m_s, b_s, p_s, q_s = terms
    C = CHUNK
    width = heads * DK
    rows = lax.broadcasted_iota(jnp.int32, (C, C), 0)
    cols = lax.broadcasted_iota(jnp.int32, (C, C), 1)
    tril = jnp.where(rows >= cols, 1.0, 0.0).astype(jnp.bfloat16)
    eye = jnp.where(rows == cols, 1.0, 0.0)
    total = conv.shape[1] // 3

    def part(t, chunk, h):
        at = pl.multiple_of(t * total + me * width + h * DK, DK)
        acc = None
        near = mixed_s[pl.ds(pl.multiple_of(chunk * C, C), C + 8), t * width + h * DK : t * width + (h + 1) * DK]
        for j in range(CONV):
            got = near[8 - (CONV - 1) + j : 8 - (CONV - 1) + j + C]
            term = conv[j : j + 1, pl.ds(at, DK)] * got
            acc = term if acc is None else acc + term
        return acc * sigmoid(acc)

    def unit(a):
        return a * lax.rsqrt(jnp.sum(a * a, axis=-1, keepdims=True) + 1e-06)

    stage = []
    for chunk, h in places:
        q = unit(part(0, chunk, h)) * DK ** (-0.5)
        k = unit(part(1, chunk, h))
        v = part(2, chunk, h)
        at = pl.multiple_of(me * width + h * DK, DK)
        down = low_s[pl.ds(pl.multiple_of(chunk * C, C), C), :DK]
        logdec = -rate[:, pl.ds(at, DK)] * sigmoid(mm(down, du[:, pl.ds(at, DK)]))
        every = beta_s[pl.ds(pl.multiple_of(chunk * C, C), C), :]
        lane = lax.broadcasted_iota(jnp.int32, every.shape, 1)
        beta = jnp.sum(jnp.where(lane == me * heads + h, every, 0.0), axis=1, keepdims=True)
        lh, ll = split(logdec)
        ls = mm(tril, lh) + mm(tril, ll)
        last = ls[C - 1 : C, :]
        grow = jnp.exp(ls)
        kup = k * grow
        stage.append((kup, k * jnp.exp(-ls), q * grow, k * jnp.exp(last - ls), v, beta, jnp.exp(last)))
    cut, dot = product(LEVELS["g"])
    lowers, attends = [], []
    for kup, kdown, qup, kend, v, beta, dec in stage:
        kd = cut(kdown)
        lowers.append(jnp.where(rows > cols, dot(cut(kup), kd, NT) * beta, 0.0))
        attends.append(jnp.where(rows >= cols, dot(cut(qup), kd, NT), 0.0))
    cut, dot = product(LEVELS["t"])
    inverse = [eye - jnp.where(rows // 2 == cols // 2, low_, 0.0) for low_ in lowers]
    size = 2
    while size < C:
        mask = jnp.logical_and(rows // (2 * size) == cols // (2 * size), rows // size != cols // size)
        ts = [cut(t) for t in inverse]
        mid = [dot(cut(jnp.where(mask, low_, 0.0)), t) for low_, t in zip(lowers, ts)]
        inverse = [t - dot(tc, cut(x)) for t, tc, x in zip(inverse, ts, mid)]
        size *= 2
    cut, dot = product(LEVELS["s"])
    solved = []
    for t, (kup, kdown, qup, kend, v, beta, dec) in zip(inverse, stage):
        tc = cut(t)
        solved.append((dot(tc, cut(v * beta)), dot(tc, cut(kup * beta))))
    cut, dot = product(LEVELS["m"])
    for (chunk, h), (vw, kw), at, (kup, kdown, qup, kend, v, beta, dec) in zip(places, solved, attends, stage):
        vc, kc, ac, ec = cut(vw), cut(kw), cut(at), cut(kend)
        slot = chunk * heads + h
        p_s[slot] = dot(ac, vc)
        q_s[slot] = qup - dot(ac, kc)
        m_s[slot] = eye * dec - dot(ec, kc, TN)
        b_s[slot] = dot(ec, vc, TN)


def run_states(chunks, me, heads, refs, low_s, terms, states, put, post):
    gu, gain = refs
    m_s, b_s, p_s, q_s = terms
    C = CHUNK
    width = heads * DK
    cut, dot = product(LEVELS["c"])

    def step(chunk):
        for h in range(heads):
            slot = chunk * heads + h
            s = cut(states[h])
            core = p_s[slot] + dot(cut(q_s[slot]), s)
            states[h] = dot(cut(m_s[slot]), s) + b_s[slot]
            at = pl.multiple_of(me * width + h * DK, DK)
            gate = sigmoid(mm(low_s[pl.ds(pl.multiple_of(chunk * C, C), C), DK:], gu[:, pl.ds(at, DK)]))
            core = core * lax.rsqrt(jnp.mean(core * core, axis=-1, keepdims=True) + 1e-06) * gain[...]
            put(chunk, h, low(core * gate))
        post(chunk)

    for chunk in chunks:
        step(chunk)


MESH = pl.DeviceIdType.MESH


def ring_place(device, n):
    return jnp.where(device % 2 == 0, device // 2, n - 1 - device // 2)


def ring_device(place, n):
    return jnp.where(place < n // 2, 2 * place, 2 * (n - 1 - place) + 1)


def greet(n):
    me, rep = lax.axis_index("seq"), lax.axis_index("rep")
    barrier = pltpu.get_barrier_semaphore()
    for k in range(1, n):
        pl.semaphore_signal(barrier, inc=1, device_id={"seq": (me + k) % n}, device_id_type=MESH)
    for other in ((rep + 2) % 4, rep + 1 - 2 * (rep % 2)):
        pl.semaphore_signal(barrier, inc=1, device_id={"rep": other}, device_id_type=MESH)
    pl.semaphore_wait(barrier, n + 1)


def remote(src, dst, sems, k, to):
    return pltpu.make_async_remote_copy(
        src_ref=src, dst_ref=dst, send_sem=sems[0].at[k], recv_sem=sems[1].at[k], device_id=to, device_id_type=MESH
    )


def ring_copies(n, blocks, sems):
    me = lax.axis_index("seq")
    place = ring_place(me, n)
    right = {"seq": ring_device((place + 1) % n, n)}
    left = {"seq": ring_device((place + n - 1) % n, n)}
    half = blocks.shape[1] // 2
    steps = []
    for k in range(n // 2):
        goes_right = blocks.at[ring_device((place + n - k) % n, n)]
        goes_left = blocks.at[ring_device((place + k) % n, n)]
        comes_left = blocks.at[ring_device((place + n - k - 1) % n, n)]
        comes_right = blocks.at[ring_device((place + k + 1) % n, n)]
        if k == n // 2 - 1:
            goes_right, comes_left = goes_right.at[pl.ds(0, half)], comes_left.at[pl.ds(0, half)]
            goes_left, comes_right = goes_left.at[pl.ds(half, half)], comes_right.at[pl.ds(half, half)]
        steps.append(
            (
                remote(goes_right, goes_right, sems, 2 * k, right),
                remote(goes_left, goes_left, sems, 2 * k + 1, left),
                remote(comes_left, comes_left, sems, 2 * k, left),
                remote(comes_right, comes_right, sems, 2 * k + 1, right),
            )
        )
    return steps


class WeightMoves:
    def __init__(self, n, source, held, sems, local_sems):
        self.n, self.held = n, held
        me, rep = lax.axis_index("seq"), lax.axis_index("rep")
        width = held.shape[2]
        share = held.shape[1] // 4
        inverse = pow(3, -1, n)
        across, beside = (rep + 2) % 4, rep + 1 - 2 * (rep % 2)
        rows = lambda r: pl.ds(pl.multiple_of(r * share, 16), share)
        self.out, self.sent_here, self.came_here, self.local = [], [], [], []
        self.to_across, self.to_beside, self.onward = [], [], []
        self.from_across, self.from_beside, self.from_onward = [], [], []
        for j in range(3):
            piece = source.at[rows(rep), j * width : (j + 1) * width]
            mine = held.at[j, rows(rep)]
            to = (3 * me + j) % n
            self.sent_here.append(to == me)
            self.came_here.append((inverse * (me + n - j)) % n == me)
            self.out.append(remote(piece, mine, sems, j, {"seq": to}))
            self.local.append(pltpu.make_async_copy(piece, mine, local_sems.at[j]))
            self.to_across.append(remote(mine, mine, sems, 3 + j, {"rep": across}))
            self.to_beside.append(remote(mine, mine, sems, 6 + j, {"rep": beside}))
            over = held.at[j, rows(across)]
            self.from_across.append(remote(over, over, sems, 3 + j, {"rep": across}))
            self.onward.append(remote(over, over, sems, 9 + j, {"rep": beside}))
            near = held.at[j, rows(beside)]
            self.from_beside.append(remote(near, near, sems, 6 + j, {"rep": beside}))
            far = held.at[j, rows((beside + 2) % 4)]
            self.from_onward.append(remote(far, far, sems, 9 + j, {"rep": beside}))

    def begin(self):
        for j in range(3):
            pl.when(self.sent_here[j])(self.local[j].start)
            pl.when(jnp.logical_not(self.sent_here[j]))(self.out[j].start)

    def spread(self):
        for j in range(3):
            pl.when(self.came_here[j])(self.local[j].wait)
            pl.when(jnp.logical_not(self.came_here[j]))(self.out[j].wait_recv)
            self.to_across[j].start()
            self.to_beside[j].start()

    def pass_on(self):
        for j in range(3):
            self.from_across[j].wait_recv()
            self.onward[j].start()

    def finish(self):
        for j in range(3):
            self.from_beside[j].wait_recv()
            self.from_onward[j].wait_recv()

    def sent(self):
        for j in range(3):
            pl.when(jnp.logical_not(self.sent_here[j]))(self.out[j].wait_send)
            self.to_across[j].wait_send()
            self.to_beside[j].wait_send()
            self.onward[j].wait_send()


def gather_kernel(n, tok, w, blocks, held, tok_send, tok_recv, w_send, w_recv, local):
    me = lax.axis_index("seq")
    own = pltpu.make_async_copy(tok, blocks.at[me], local.at[3])
    own.start()
    greet(n)
    moves = WeightMoves(n, w, held, (w_send, w_recv), local)
    moves.begin()
    own.wait()
    steps = ring_copies(n, blocks, (tok_send, tok_recv))
    for k, (right, left, came_left, came_right) in enumerate(steps):
        right.start()
        left.start()
        if k == 0:
            moves.spread()
        if k == 2:
            moves.pass_on()
        came_left.wait_recv()
        came_right.wait_recv()
    moves.finish()
    moves.sent()
    for right, left, came_left, came_right in steps:
        right.wait_send()
        left.wait_send()


def gathered(tokens, qkv_weight, n, width):
    depth = qkv_weight.shape[0]
    anywhere = pl.BlockSpec(memory_space=pl.ANY)
    return pl.pallas_call(
        functools.partial(gather_kernel, n),
        out_shape=[
            jax.ShapeDtypeStruct((n,) + tokens.shape, tokens.dtype),
            jax.ShapeDtypeStruct((3, depth, width), qkv_weight.dtype),
        ],
        in_specs=[anywhere] * 2,
        out_specs=[anywhere] * 2,
        scratch_shapes=[
            pltpu.SemaphoreType.DMA((n,)),
            pltpu.SemaphoreType.DMA((n,)),
            pltpu.SemaphoreType.DMA((12,)),
            pltpu.SemaphoreType.DMA((12,)),
            pltpu.SemaphoreType.DMA((4,)),
        ],
        compiler_params=pltpu.CompilerParams(collective_id=0, has_side_effects=True),
    )(tokens, qkv_weight)


def heads_kernel(n, heads, tok, w, conv, dd, du, rate, bw, bs, gd, gu, gain, out, mixed_s, low_s, beta_s, m_s, b_s, p_s, q_s, states, stage, send, recv, local):
    me = lax.axis_index("seq")
    count = tok.shape[0]
    chunks = count // CHUNK
    width = heads * DK
    greet(n)
    mixed_s[0:8, :] = jnp.zeros((8, mixed_s.shape[1]), jnp.float32)

    def w_at(t):
        return w[lax.rem(t * n + me, 3)]

    def first(c, carry):
        rows = pl.multiple_of(c * CHUNK, CHUNK)
        project(rows, tok[pl.ds(rows, CHUNK), :], w_at, (dd, gd, bw, bs), mixed_s, low_s, beta_s)
        return carry

    lax.fori_loop(0, chunks, first, 0)

    def columns(device):
        return out.at[:, pl.ds(pl.multiple_of(device * width, width), width)]

    def parcel(to):
        return pltpu.make_async_remote_copy(
            src_ref=stage.at[to], dst_ref=columns(me), send_sem=send.at[to], recv_sem=recv.at[me],
            device_id={"seq": to}, device_id_type=MESH,
        )

    def put(chunk, h, value):
        stage[chunk, :, h * DK : (h + 1) * DK] = value

    def post(chunk):
        pl.when(chunk != me)(lambda: parcel(chunk).start())

    for h in range(heads):
        states[h] = jnp.zeros((DK, DK), jnp.float32)

    def second(c, carry):
        pair = [c * 2, c * 2 + 1]
        terms = (m_s, b_s, p_s, q_s)
        places = [(chunk, h) for chunk in pair for h in range(heads)]
        chunk_terms(places, me, heads, (conv, du, rate), (mixed_s, low_s, beta_s), terms)
        run_states(pair, me, heads, (gu, gain), low_s, terms, states, put, post)
        return carry

    lax.fori_loop(0, chunks // 2, second, 0)
    own = pltpu.make_async_copy(stage.at[me], columns(me), local.at[0])
    own.start()
    own.wait()
    for k in range(1, n):
        other = (me + k) % n
        parcel(other).wait_send()
        pltpu.make_async_remote_copy(
            src_ref=stage.at[other], dst_ref=columns(other), send_sem=send.at[other], recv_sem=recv.at[other],
            device_id={"seq": other}, device_id_type=MESH,
        ).wait_recv()


def heads_split(tokens, qkv_weight, conv_weight, decay_down, decay_up, decay_rate, beta_weight, beta_scale, gate_down, gate_up, norm_gain):
    n = lax.axis_size("seq")
    heads = H // n
    width = heads * DK
    blocks, weight = gathered(tokens, qkv_weight, n, width)
    everything = blocks.reshape(-1, tokens.shape[1])
    count = everything.shape[0]
    slots = count // CHUNK * heads
    square = pltpu.VMEM((slots, DK, DK), jnp.float32)
    attended = pl.pallas_call(
        functools.partial(heads_kernel, n, heads),
        out_shape=jax.ShapeDtypeStruct((tokens.shape[0], H * DK), jnp.bfloat16),
        in_specs=[pl.BlockSpec(memory_space=pltpu.VMEM)] * 11,
        out_specs=pl.BlockSpec(memory_space=pltpu.VMEM),
        scratch_shapes=[
            pltpu.VMEM((count + 8, 3 * width), jnp.float32),
            pltpu.VMEM((count, 2 * DK), jnp.bfloat16),
            pltpu.VMEM((count, H), jnp.float32),
            square, square, square, square,
            pltpu.VMEM((heads, DK, DK), jnp.float32),
            pltpu.VMEM((n, CHUNK, width), jnp.bfloat16),
            pltpu.SemaphoreType.DMA((n,)),
            pltpu.SemaphoreType.DMA((n,)),
            pltpu.SemaphoreType.DMA((1,)),
        ],
        compiler_params=pltpu.CompilerParams(collective_id=1, has_side_effects=True, vmem_limit_bytes=48 * 2**20),
    )(everything, weight, conv_weight, decay_down, decay_up, decay_rate.reshape(1, -1), beta_weight, beta_scale.reshape(1, -1), gate_down, gate_up, norm_gain.reshape(1, -1))
    return attended


def layer(tokens, *rest):
    n, reps = lax.axis_size("seq"), lax.axis_size("rep")
    fits = H % n == 0 and n % 3 != 0 and n % 2 == 0 and reps == 4 and tokens.shape[0] == CHUNK
    return (heads_split if fits else tokens_split)(tokens, *rest)


def solution(mesh):
    in_specs = (
        P(("rep", "seq"), None),
        P(None, "seq"),
        P(),
        P(),
        P(),
        P(),
        P(),
        P(),
        P(),
        P(),
        P(),
    )
    out_specs = P(("rep", "seq"), None)
    return jax.shard_map(
        layer, mesh=mesh, in_specs=in_specs, out_specs=out_specs, check_vma=False
    )
```
